32 devices in a mesh: row: 16 (over z, x, core), col: 2 (over y).
Axes of the slice: x: 2, y: 2, z: 4, core: 2. Of those that a mesh axis runs over, the one named last changes fastest.
Arguments:
- sigma_anc: float32 [64, 64, 128, 128], P('row', 'col'), as said below
- panel: float32 [2, 64, 128, 512], P(None, 'row'), may hold values from -0.12 to 0.12
- pattern: int32 [2, 32], replicated, may hold values from 0 to 63, as said below
- linv: float32 [2, 512, 512], replicated, as said below
Outputs:
- sigma_sj: float32 [2, 64, 128, 512], P(None, 'row')
- sigma_jj: float32 [2, 512, 512], replicated
The draws below stay inside these ranges and needn't reach their ends.
Inputs may be any that keep to these rules, and one draw needn't show every extreme that they name: `pattern`: each row lists 32 distinct ancestor block indices in increasing order; 0 and 63 are always among them. `sigma_anc`: symmetric as a matrix of order 64 * 128 in ancestor order. `linv`: lower triangular, diagonal entries between 1 and 2.
All inputs are finite; a program needn't handle non-finite values.
Results may differ from the reference program's by a relative error of at most 0.0001.
Values sent between devices are 32-bit elements; how exact they have to be, the bound alone decides.
No kernel may reach another device: no remote copies, remote signals or barrier semaphores. Data moves between devices by JAX's collectives and lax.ppermute only.
A program may use at most 128 MiB of HBM per device.

```python
import jax
import jax.numpy as jnp
from jax import lax

W = 512
BS = 128
SUPER = 2
QR = 4
NB = 64
QC = 32
KS = 32
N_ROW = 16
N_COL = 2


def draw_sigma_anc(key, part):
    first, second = jax.random.split(key, 2)
    order = NB * BS
    base = jax.random.normal(first, (NB, NB, BS, BS), jnp.float32)
    full = (base + jnp.transpose(base, (1, 0, 3, 2))) * (1.4142135 / jnp.sqrt(jnp.float32(order)))
    diag_values = jax.random.uniform(second, (NB, BS), jnp.float32, 1.0, 4.0)
    block_eye = jnp.eye(NB, dtype=jnp.float32)[:, :, None, None]
    inner_eye = jnp.eye(BS, dtype=jnp.float32)[None, None, :, :]
    full = full + block_eye * inner_eye * diag_values[:, None, :, None]
    storage = jnp.arange(NB, dtype=jnp.int32)
    row_map = storage % QR * N_ROW + storage // QR
    col_map = storage % QC * N_COL + storage // QC
    return full[row_map][:, col_map]


def draw_pattern(key, part):
    keys = jax.random.split(key, SUPER)

    def single(one_key):
        inner = (jax.random.permutation(one_key, NB - 2)[:KS - 2] + 1).astype(jnp.int32)
        ends = jnp.array([0, NB - 1], dtype=jnp.int32)
        return jnp.sort(jnp.concatenate([ends, inner]))
    return jax.vmap(single)(keys).astype(jnp.int32)


def draw_linv(key, part):
    first, second = jax.random.split(key)
    lower = jax.random.normal(first, (SUPER, W, W), jnp.float32) / jnp.sqrt(jnp.float32(W))
    diagonal = jax.random.uniform(second, (SUPER, W), jnp.float32, 1.0, 2.0)
    return jnp.tril(lower, -1) + diagonal[:, :, None] * jnp.eye(W, dtype=jnp.float32)[None]


def level_of(rng, shape, shards, low, top_value):
    level, own = 1.0, jax.random.fold_in(rng, 6)
    for dim, shards_of in shards:
        steps = jnp.exp(jax.random.uniform(jax.random.fold_in(own, dim), (shards_of,), jnp.float32, low / len(shards), top_value / len(shards)))
        level = level * jnp.repeat(steps, shape[dim] // shards_of).reshape([-1 if axis == dim else 1 for axis in range(len(shape))])
    return level


def normal_values(own_key, shape, width, bound, pieces=(), kind=jnp.bfloat16):
    result = width * jax.random.normal(own_key, shape, jnp.float32)
    if pieces:
        result = result * level_of(own_key, shape, pieces, -0.22, 0.18)
    return jnp.clip(result, -bound, bound).astype(kind)


def setup_inputs(seed: int = 0) -> dict:
    arg_keys = jax.random.split(jax.random.key(seed), 5)
    return {
        "sigma_anc": draw_sigma_anc(jax.random.fold_in(arg_keys[4], 71), 0),
        "panel": normal_values(arg_keys[1], (SUPER, NB, BS, W), 0.02, 0.12, ((1, 16),), jnp.float32),
        "pattern": draw_pattern(jax.random.fold_in(arg_keys[4], 71), 0),
        "linv": draw_linv(jax.random.fold_in(arg_keys[4], 71), 0),
    }


def reference(sigma_anc, panel, pattern, linv):
    highest = lax.Precision.HIGHEST
    sj_list = []
    jj_list = []
    for number in range(SUPER):
        blocks = pattern[number].astype(jnp.int32)
        store_rows = ((blocks % N_ROW) * QR + blocks // N_ROW).astype(jnp.int32)
        store_cols = ((blocks % N_COL) * QC + blocks // N_COL).astype(jnp.int32)
        picked = sigma_anc[store_rows][:, store_cols]
        dense = jnp.transpose(picked, (0, 2, 1, 3)).reshape(KS * BS, KS * BS)
        factor = panel[number][store_rows].reshape(KS * BS, W)
        updated = jnp.dot(factor, linv[number], precision=highest, preferred_element_type=jnp.float32)
        product = jnp.dot(dense, updated, precision=highest, preferred_element_type=jnp.float32)
        placed = jnp.zeros((NB, BS, W), jnp.float32).at[store_rows].set(-product.reshape(KS, BS, W))
        inner = jnp.dot(linv[number].T, linv[number], precision=highest, preferred_element_type=jnp.float32)
        inner = inner + jnp.dot(updated.T, product, precision=highest, preferred_element_type=jnp.float32)
        sj_list.append(placed)
        jj_list.append(inner)
    return jnp.stack(sj_list), jnp.stack(jj_list)
```

```python
import functools

import jax
import jax.numpy as jnp
from jax import lax
from jax.experimental import pallas as pl
from jax.experimental.pallas import tpu as pltpu
from jax.sharding import PartitionSpec as P

F32 = jnp.float32
BF16 = jnp.bfloat16
MIB = 1 << 20


def split(x):
    hi = x.astype(BF16)
    return hi, (x - hi.astype(F32)).astype(BF16)


def dot3(a, b, dims=(((1,), (0,)), ((), ()))):
    dot = functools.partial(lax.dot_general, dimension_numbers=dims, preferred_element_type=F32)
    return dot(a[0], b[0]) + (dot(a[0], b[1]) + dot(a[1], b[0]))


ITEMS = 8
TRANSPOSED = (((0,), (0,)), ((), ()))


def in_vmem(count):
    return [pl.BlockSpec(memory_space=pltpu.VMEM)] * count


def params(mib=24):
    return pltpu.CompilerParams(vmem_limit_bytes=mib * MIB)


def update_kernel(core, panel, linv, near, away):
    supers, rows, size, width = panel.shape
    half = width // 2
    swapped = core[0] == 1
    for j in range(supers):
        left = split(panel[j].reshape(rows * size, width))
        low = split(linv[j, :, :half])
        high = split(linv[j, half:, half:])
        first = dot3(left, low)
        second = dot3((left[0][:, half:], left[1][:, half:]), high)
        here, there = jnp.where(swapped, second, first), jnp.where(swapped, first, second)
        near[j * rows:(j + 1) * rows] = here.reshape(rows, size, half)
        away[j * rows:(j + 1) * rows] = there.reshape(rows, size, half)


def update(core, panel, linv):
    supers, rows, size, width = panel.shape
    return pl.pallas_call(
        update_kernel,
        grid_spec=pltpu.PrefetchScalarGridSpec(
            num_scalar_prefetch=1, grid=(), in_specs=in_vmem(2), out_specs=in_vmem(2)
        ),
        out_shape=[jax.ShapeDtypeStruct((ITEMS, size, width // 2), F32)] * 2,
        compiler_params=params(),
        cost_estimate=pl.CostEstimate(
            flops=6 * supers * rows * size * width * width, bytes_accessed=6 * MIB, transcendentals=0
        ),
        name="update",
    )(core, panel, linv)


def column_kernel(wanted, chip, u0, u1, own, oth, acc, out, blocks, arrived):
    rows, cols, size, _ = own.shape
    items, _, width = u0.shape

    def copy(i, source):
        ref = (own, oth)[source]
        column = i * (cols // items) + chip[0]
        return pltpu.make_async_copy(ref.at[:, column], blocks.at[i, source], arrived.at[i, source])

    def wants(i):
        at = chip[0] * ITEMS + i
        return wanted[at] != 0, wanted[at + items] != 0

    for i in range(items):
        first, second = wants(i)

        @pl.when(first | second)
        def _():
            copy(i, 0).start()
            copy(i, 1).start()

    out[...] = acc[...]

    def body(i, carry):
        first, second = wants(i)

        @pl.when(first | second)
        def _():
            pair = [jnp.where(first, u0[i], 0.0), jnp.where(second, u1[i], 0.0)]
            high, low = split(jnp.concatenate(pair, axis=1))
            twice = jnp.concatenate([high, high], axis=0)
            for source in range(2):
                copy(i, source).wait()
                left = split(blocks[i, source].reshape(rows * size, size))
                product = jnp.dot(jnp.concatenate(left, axis=1), twice, preferred_element_type=F32)
                product += jnp.dot(left[0], low, preferred_element_type=F32)
                for j in range(2):
                    out[j, source] += product[:, j * width:(j + 1) * width].reshape(rows, size, width)

        return carry

    lax.fori_loop(0, items, body, 0)


def add_columns(wanted, chip, u0, u1, own, oth, acc):
    items, size, width = u0.shape
    rows = own.shape[0]
    far = pl.BlockSpec(memory_space=pltpu.HBM)
    return pl.pallas_call(
        column_kernel,
        grid_spec=pltpu.PrefetchScalarGridSpec(
            num_scalar_prefetch=2,
            grid=(),
            in_specs=in_vmem(2) + [far, far] + in_vmem(1),
            out_specs=pl.BlockSpec(memory_space=pltpu.VMEM),
            scratch_shapes=[
                pltpu.VMEM((items, 2, rows, size, size), F32),
                pltpu.SemaphoreType.DMA((items, 2)),
            ],
        ),
        out_shape=jax.ShapeDtypeStruct(acc.shape, F32),
        input_output_aliases={6: 0},
        compiler_params=params(20),
        cost_estimate=pl.CostEstimate(
            flops=24 * items * rows * size * size * width, bytes_accessed=6 * MIB, transcendentals=0
        ),
        name="add_columns",
    )(wanted, chip, u0, u1, own, oth, acc)


def inner_kernel(wanted, core, near, away, near_oth, away_oth, share, y, out):
    supers, _, rows, size, half = y.shape
    for j in range(supers):
        low, high = share[j, :, :half], share[j, :, half:]
        here, there = jnp.where(core[0] == 1, high, low), jnp.where(core[0] == 1, low, high)

        def stack(start, pair):
            parts = [ref[j * rows:(j + 1) * rows].reshape(rows * size, half) for ref in pair]
            return split(jnp.concatenate(parts + [start], axis=0))

        right = [
            jnp.where(wanted[source * ITEMS + j * rows + q] != 0, y[j, source, q], 0.0)
            for source in range(2)
            for q in range(rows)
        ]
        right = split(jnp.concatenate(right + [here], axis=0))
        diag = dot3(stack(here, (near, near_oth)), right, TRANSPOSED)
        out[3 * j] = diag[:size, :size]
        out[3 * j + 1] = diag[size:, :size]
        out[3 * j + 2] = diag[size:, size:]

        @pl.when(core[0] == j)
        def _():
            cross = dot3(stack(there, (away, away_oth)), right, TRANSPOSED)
            for a in range(2):
                for b in range(2):
                    out[6 + 2 * a + b] = cross[a * size:(a + 1) * size, b * size:(b + 1) * size]


def inner(wanted, core, near, away, near_oth, away_oth, share, y):
    supers, _, rows, size, half = y.shape
    return pl.pallas_call(
        inner_kernel,
        grid_spec=pltpu.PrefetchScalarGridSpec(
            num_scalar_prefetch=2,
            grid=(),
            in_specs=in_vmem(6),
            out_specs=pl.BlockSpec(memory_space=pltpu.VMEM),
        ),
        out_shape=jax.ShapeDtypeStruct((10, size, size), F32),
        compiler_params=params(32),
        cost_estimate=pl.CostEstimate(
            flops=36 * rows * size * half * half, bytes_accessed=8 * MIB, transcendentals=0
        ),
        name="inner",
    )(wanted, core, near, away, near_oth, away_oth, share, y)


def square_kernel(core, mine, oth, out):
    size = mine.shape[1]
    for j in range(2):
        for c in range(2):
            def tile(k):
                return jnp.where(core[0] == c, mine[k], oth[k])
            lo, mid, hi = 2 * c * size, (2 * c + 1) * size, (2 * c + 2) * size
            below = tile(3 * j + 1)
            out[j, lo:mid, lo:mid] = tile(3 * j)
            out[j, mid:hi, lo:mid] = below
            out[j, lo:mid, mid:hi] = below.T
            out[j, mid:hi, mid:hi] = tile(3 * j + 2)
            if j == c:
                for a in range(2):
                    for b in range(2):
                        piece = tile(6 + 2 * a + b)
                        r, s = (2 * (1 - c) + a) * size, (2 * c + b) * size
                        out[j, r:r + size, s:s + size] = piece
                        out[j, s:s + size, r:r + size] = piece.T


def square(core, mine, oth):
    size = mine.shape[1]
    return pl.pallas_call(
        square_kernel,
        grid_spec=pltpu.PrefetchScalarGridSpec(
            num_scalar_prefetch=1, grid=(), in_specs=in_vmem(2), out_specs=pl.BlockSpec(memory_space=pltpu.VMEM)
        ),
        out_shape=jax.ShapeDtypeStruct((2, 4 * size, 4 * size), F32),
        compiler_params=params(),
        cost_estimate=pl.CostEstimate(flops=0, bytes_accessed=4 * MIB, transcendentals=0),
        name="square",
    )(core, mine, oth)


def place_kernel(wanted, core, one0, one1, two0, two1, oth0, oth1, out):
    half = one0.shape[2]
    e = pl.program_id(0)
    rows = pl.num_programs(0) // 2

    @pl.when(wanted[e] == 0)
    def _():
        out[...] = jnp.zeros_like(out)

    for j, (one, two, oth) in enumerate(((one0, two0, oth0), (one1, two1, oth1))):

        @pl.when((wanted[e] != 0) & (e // rows == j))
        def _():
            mine = one[0] + two[0]
            other = oth[0]
            out[0, 0, :, :half] = -jnp.where(core[0] == 0, mine, other)
            out[0, 0, :, half:] = -jnp.where(core[0] == 0, other, mine)


def place(wanted, core, one, two, oth):
    rows, size, half = one[0].shape
    in_specs = [
        pl.BlockSpec((1, size, half), lambda e, *_: (jnp.minimum(e, rows - 1), 0, 0)),
        pl.BlockSpec((1, size, half), lambda e, *_: (jnp.maximum(e - rows, 0), 0, 0)),
    ]
    return pl.pallas_call(
        place_kernel,
        grid_spec=pltpu.PrefetchScalarGridSpec(
            num_scalar_prefetch=2,
            grid=(ITEMS,),
            in_specs=in_specs * 3,
            out_specs=pl.BlockSpec((1, 1, size, 2 * half), lambda e, *_: (e // rows, e % rows, 0, 0)),
        ),
        out_shape=jax.ShapeDtypeStruct((2, rows, size, 2 * half), F32),
        compiler_params=params(),
        cost_estimate=pl.CostEstimate(flops=0, bytes_accessed=5 * MIB, transcendentals=0),
        name="place",
    )(wanted, core, *one, *two, *oth)


def any_mesh(sigma_anc, panel, pattern, linv):
    high = lax.Precision.HIGH
    einsum = functools.partial(jnp.einsum, precision=high, preferred_element_type=F32)
    rows, cols = lax.axis_size("row"), lax.axis_size("col")
    row_ids = jnp.arange(sigma_anc.shape[0], dtype=jnp.int32) * rows + lax.axis_index("row")
    col_ids = jnp.arange(sigma_anc.shape[1], dtype=jnp.int32) * cols + lax.axis_index("col")
    wanted = jnp.any(pattern[:, :, None] == row_ids, axis=1).astype(F32)[:, :, None, None]
    u = einsum("sqiw,swv->sqiv", panel, linv) * wanted
    pick = (col_ids[:, None] == row_ids[None, :]).astype(F32)
    u_cols = lax.psum(jnp.einsum("kq,sqiw->skiw", pick, u, precision=lax.Precision.HIGHEST), "row")
    y = lax.psum(einsum("qkij,skjw->sqiw", sigma_anc, u_cols), "col") * wanted
    total = lax.psum(einsum("sqiw,sqiv->swv", u, y), "row")
    return -y, einsum("siw,siv->swv", linv, linv) + total


def ring_place(chip, chips):
    z, x = chip // 2, chip % 2
    return jnp.where(x == 0, z, chips - 1 - z)


def ring_chip(place, chips):
    place = place % chips
    return jnp.where(place < chips // 2, 2 * place, 2 * (chips - 1 - place) + 1)


def pair_rows(sigma_anc, panel, linv, wanted):
    supers, rows, size, width = panel.shape
    half = width // 2
    n_row = lax.axis_size("row")
    chips = n_row // 2
    me, plane = lax.axis_index("row"), lax.axis_index("col")
    chip, core = me // 2, me % 2
    place_here = ring_place(chip, chips)
    across = [(i, i ^ 1) for i in range(n_row)]
    pair = [(0, 1), (1, 0)]
    order = [2 * q for q in range(chips // 2)] + [2 * (chips - 1 - q) + 1 for q in range(chips // 2, chips)]
    around = []
    for q in range(chips):
        around.append((2 * order[q], 2 * order[(q + 1) % chips]))
        around.append((2 * order[q] + 1, 2 * order[(q - 1) % chips] + 1))

    near, away = update(core[None], panel, linv)
    away_oth = lax.ppermute(away, "row", across)
    first = jnp.where(core == plane, near, away_oth)
    wanted_here = jnp.where(plane == 0, wanted[0], wanted[1]).reshape(-1)
    wanted_rows = jnp.where(core == 0, wanted, wanted[::-1])
    wanted_rows = lax.dynamic_index_in_dim(wanted_rows, chip, 1, keepdims=False).reshape(-1)
    held = [first[:rows], first[rows:]]
    acc = jnp.zeros((supers, 2, rows, size, half), F32)
    waiting = []
    s_own = pltpu.with_memory_space_constraint(sigma_anc, pltpu.HBM)
    s_oth = near_oth = None
    for step in range(chips):
        origin = ring_chip(place_here + jnp.where(core == 0, -step, step), chips)
        blocks = tuple(held)
        if step < chips - 1:
            held[0] = lax.ppermute(held[0], "row", around)
            while len(waiting) > (step < chips // 2):
                acc = add_columns(*waiting.pop(0), acc)
            sent, acc = lax.optimization_barrier((held[1], acc))
            held[1] = lax.ppermute(sent, "row", around)
        if s_oth is None:
            s_sent, near_sent, _ = lax.optimization_barrier((sigma_anc, near, away_oth))
            s_oth = lax.ppermute(s_sent, "row", across)
            near_oth = lax.ppermute(near_sent, "row", across)
        waiting.append((wanted_here, origin[None], *blocks, s_own, s_oth))
    for last in waiting:
        acc = add_columns(*last, acc)

    span = width // (2 * chips)
    share = lax.dynamic_slice_in_dim(linv, (chip * 2 + plane) * span, span, axis=1)
    part = inner(wanted_rows, core[None], near, away, away_oth, near_oth, share, acc)
    recv0 = [lax.ppermute(acc[0][source], "col", pair) for source in (1, 0)]
    total, recv0, recv1 = all_sum(part, recv0, acc[1], chip, chips, pair)
    recv = (recv0, recv1)
    y_oth = [lax.ppermute(acc[j][1] + recv[j][0], "row", across) for j in range(supers)]
    total_oth = lax.ppermute(total, "row", across)
    sigma_sj = place(
        wanted_rows[:ITEMS], core[None], [a[0] for a in acc], [r[1] for r in recv], y_oth
    )
    return sigma_sj, square(core[None], total, total_oth)


def all_sum(x, first, second, chip, chips, pair):
    shape = x.shape
    flat = x.reshape(-1, shape[-1])
    h = flat.shape[0] // chips

    def flip(bits):
        return [(i, i ^ (2 * bits)) for i in range(2 * chips)]

    mine = lax.dynamic_slice_in_dim(flat, chip * h, h)
    for bits in range(1, chips):
        sent = lax.dynamic_slice_in_dim(flat, (chip ^ bits) * h, h)
        mine = mine + lax.ppermute(sent, "row", flip(bits))
    mine, *first = lax.optimization_barrier((mine, *first))
    mine = mine + lax.ppermute(mine, "col", pair)
    second, mine = lax.optimization_barrier((second, mine))
    second = [lax.ppermute(second[source], "col", pair) for source in (1, 0)]
    came = [mine] + [lax.ppermute(mine, "row", flip(bits)) for bits in range(1, chips)]
    total = jnp.concatenate([lax.select_n(chip ^ p, *came) for p in range(chips)])
    return total.reshape(shape), first, second


def local(sigma_anc, panel, pattern, linv):
    n_row, n_col = lax.axis_size("row"), lax.axis_size("col")
    rows = sigma_anc.shape[0]
    supers = panel.shape[0]
    if (n_row, n_col, rows * supers) != (16, 2, ITEMS):
        return any_mesh(sigma_anc, panel, pattern, linv)
    chips = n_row // 2
    e = jnp.arange(ITEMS, dtype=jnp.int32)
    ids = (
        (e % rows)[None, None, :] * n_row
        + 2 * jnp.arange(chips, dtype=jnp.int32)[None, :, None]
        + jnp.arange(2, dtype=jnp.int32)[:, None, None]
    )
    hit = jnp.any(pattern[:, None, None, None, :] == ids[None, ..., None], axis=-1)
    wanted = jnp.where(e // rows == 0, hit[0], hit[1])
    return pair_rows(sigma_anc, panel, linv, wanted.astype(jnp.int32))


def solution(mesh):
    return jax.shard_map(
        local,
        mesh=mesh,
        in_specs=(P("row", "col", None, None), P(None, "row", None, None), P(), P()),
        out_specs=(P(None, "row", None, None), P()),
        check_vma=False,
    )
```

```python
import functools

import jax
import jax.numpy as jnp
from jax import lax
from jax.experimental import pallas as pl
from jax.experimental.pallas import tpu as pltpu
from jax.sharding import PartitionSpec as P

F32 = jnp.float32
BF16 = jnp.bfloat16
MIB = 1 << 20


def split(x):
    hi = x.astype(BF16)
    return hi, (x - hi.astype(F32)).astype(BF16)


def dot3(a, b, a_axis=1, b_axis=0):
    left = jnp.concatenate([a[0], a[1], a[0]], axis=a_axis)
    right = jnp.concatenate([b[0], b[0], b[1]], axis=b_axis)
    dims = (((a_axis,), (b_axis,)), ((), ()))
    return lax.dot_general(left, right, dims, preferred_element_type=F32)


def three(a, b):
    dot = functools.partial(jnp.dot, preferred_element_type=F32)
    return dot(a[0], b[0]) + (dot(a[0], b[1]) + dot(a[1], b[0]))


ITEMS = 8
PLACES = (((1, 0), (0, 0)), ((1, 1), (0, 1)))


def in_vmem(count):
    return [pl.BlockSpec(memory_space=pltpu.VMEM)] * count


def far(x):
    return pltpu.with_memory_space_constraint(x, pltpu.HBM)


def params(mib=24):
    return pltpu.CompilerParams(vmem_limit_bytes=mib * MIB)


def update_kernel(core, panel, linv, near, away, rows_in, low_in, arrived):
    supers, rows, size, width = panel.shape
    half = width // 2
    swapped = core[0] == 1

    def copies(j):
        yield pltpu.make_async_copy(linv.at[j], low_in.at[j], arrived.at[j, rows])
        for q in range(rows):
            yield pltpu.make_async_copy(panel.at[j, q], rows_in.at[j, q], arrived.at[j, q])

    for j in range(supers):
        for copy in copies(j):
            copy.start()
    for j in range(supers):
        for copy in copies(j):
            copy.wait()
        left = split(rows_in[j].reshape(rows * size, width))
        first = three(left, split(low_in[j, :, :half]))
        second = three([x[:, half:] for x in left], split(low_in[j, half:, half:]))
        here, there = jnp.where(swapped, second, first), jnp.where(swapped, first, second)
        near[j * rows:(j + 1) * rows] = here.reshape(rows, size, half)
        away[j * rows:(j + 1) * rows] = there.reshape(rows, size, half)


def update(core, panel, linv):
    supers, rows, size, width = panel.shape
    hbm = pl.BlockSpec(memory_space=pltpu.HBM)
    return pl.pallas_call(
        update_kernel,
        grid_spec=pltpu.PrefetchScalarGridSpec(
            num_scalar_prefetch=1,
            grid=(),
            in_specs=[hbm, hbm],
            out_specs=in_vmem(2),
            scratch_shapes=[
                pltpu.VMEM(panel.shape, F32),
                pltpu.VMEM(linv.shape, F32),
                pltpu.SemaphoreType.DMA((supers, rows + 1)),
            ],
        ),
        out_shape=[jax.ShapeDtypeStruct((ITEMS, size, width // 2), F32)] * 2,
        compiler_params=params(32),
        cost_estimate=pl.CostEstimate(
            flops=6 * supers * rows * size * width * width, bytes_accessed=6 * MIB, transcendentals=0
        ),
        name="update",
    )(core, panel, linv)


def column_kernel(wanted, chip, u0, u1, own, oth, *refs):
    accs, outs, (blocks, arrived) = refs[:2], refs[2:4], refs[4:]
    rows, cols, size, _ = own.shape
    items, _, width = u0.shape

    def copy(i, source):
        ref = (own, oth)[source]
        column = i * (cols // items) + chip[0]
        return pltpu.make_async_copy(ref.at[:, column], blocks.at[i, source], arrived.at[i, source])

    def wants(i):
        at = chip[0] * ITEMS + i
        return wanted[at] != 0, wanted[at + items] != 0

    for i in range(items):
        first, second = wants(i)

        @pl.when(first | second)
        def _():
            copy(i, 0).start()
            copy(i, 1).start()

    for acc, out in zip(accs, outs):
        out[...] = acc[...]

    def body(i, carry):
        first, second = wants(i)

        @pl.when(first | second)
        def _():
            pair = [jnp.where(first, u0[i], 0.0), jnp.where(second, u1[i], 0.0)]
            right = split(jnp.concatenate(pair, axis=1))
            copy(i, 0).wait()
            copy(i, 1).wait()
            left = split(blocks[i].reshape(2 * rows * size, size))
            product = dot3(left, right).reshape(2, rows, size, 2 * width)
            for j in range(2):
                for source in range(2):
                    which, at = PLACES[j][source]
                    outs[which][at] += product[source, :, :, j * width:(j + 1) * width]

        return carry

    lax.fori_loop(0, items, body, 0)


def add_columns(wanted, chip, u0, u1, own, oth, accs):
    items, size, width = u0.shape
    rows = own.shape[0]
    hbm = pl.BlockSpec(memory_space=pltpu.HBM)
    return pl.pallas_call(
        column_kernel,
        grid_spec=pltpu.PrefetchScalarGridSpec(
            num_scalar_prefetch=2,
            grid=(),
            in_specs=in_vmem(2) + [hbm, hbm] + in_vmem(2),
            out_specs=in_vmem(2),
            scratch_shapes=[
                pltpu.VMEM((items, 2, rows, size, size), F32),
                pltpu.SemaphoreType.DMA((items, 2)),
            ],
        ),
        out_shape=[jax.ShapeDtypeStruct(acc.shape, F32) for acc in accs],
        input_output_aliases={6 + i: i for i in range(2)},
        compiler_params=params(24),
        cost_estimate=pl.CostEstimate(
            flops=24 * items * rows * size * size * width, bytes_accessed=6 * MIB, transcendentals=0
        ),
        name="add_columns",
    )(wanted, chip, u0, u1, own, oth, *accs)


def inner_kernel(wanted, core, near, away, near_oth, away_oth, share, y0, y1, out, held, arrived):
    _, rows, size, half = y0.shape
    copies = [
        pltpu.make_async_copy(ref, held.at[k], arrived.at[k])
        for k, ref in enumerate((near, near_oth, away, away_oth))
    ]
    for copy in copies:
        copy.start()

    def stack(j, k, start, begin, end):
        parts = [held[k + s, j * rows:(j + 1) * rows, :, begin:end].reshape(rows * size, end - begin) for s in range(2)]
        return split(jnp.concatenate(parts + [start[:, begin:end]], axis=0))

    for j in range(2):
        low, high = share[j, :, :half], share[j, :, half:]
        here, there = jnp.where(core[0] == 1, high, low), jnp.where(core[0] == 1, low, high)
        right = []
        for source in range(2):
            which, at = PLACES[j][source]
            for q in range(rows):
                y = (y0, y1)[which][at, q]
                right.append(jnp.where(wanted[source * ITEMS + j * rows + q] != 0, y, 0.0))
        right = split(jnp.concatenate(right + [here], axis=0))
        first = 5 * j
        if j == 0:
            copies[0].wait()
            copies[1].wait()
        diag = dot3(stack(j, 0, here, 0, half), right, 0, 0)
        out[first] = diag[:size, :size]
        out[first + 1] = diag[size:, :size]
        out[first + 2] = diag[size:, size:]
        if j == 0:
            copies[2].wait()
            copies[3].wait()

        @pl.when(core[0] == 0)
        def _():
            cross = dot3(stack(j, 2, there, 0, size), right, 0, 0)
            out[first + 3] = cross[:, :size]
            out[first + 4] = cross[:, size:]

        @pl.when(core[0] != 0)
        def _():
            cross = dot3(stack(j, 2, there, 0, half), [x[:, size:] for x in right], 0, 0)
            out[first + 3] = cross[:size]
            out[first + 4] = cross[size:]


def inner(wanted, core, near, away, near_oth, away_oth, share, ys):
    _, rows, size, half = ys[0].shape
    hbm = pl.BlockSpec(memory_space=pltpu.HBM)
    return pl.pallas_call(
        inner_kernel,
        grid_spec=pltpu.PrefetchScalarGridSpec(
            num_scalar_prefetch=2,
            grid=(),
            in_specs=[hbm] * 4 + in_vmem(3),
            out_specs=pl.BlockSpec(memory_space=pltpu.VMEM),
            scratch_shapes=[pltpu.VMEM((4, *near.shape), F32), pltpu.SemaphoreType.DMA((4,))],
        ),
        out_shape=jax.ShapeDtypeStruct((10, size, size), F32),
        compiler_params=params(36),
        cost_estimate=pl.CostEstimate(
            flops=36 * rows * size * half * half, bytes_accessed=8 * MIB, transcendentals=0
        ),
        name="inner",
    )(wanted, core, near, away, near_oth, away_oth, share, *ys)


def square_kernel(core, mine, oth, out):
    size = mine.shape[1]

    def put(j, row, col, tile):
        out[j, row * size:(row + 1) * size, col * size:(col + 1) * size] = tile

    for j in range(2):
        for c in range(2):
            diag0, below, diag1, one, two = (jnp.where(core[0] == c, mine[5 * j + k], oth[5 * j + k]) for k in range(5))
            put(j, 2 * c, 2 * c, diag0)
            put(j, 2 * c + 1, 2 * c, below)
            put(j, 2 * c, 2 * c + 1, below.T)
            put(j, 2 * c + 1, 2 * c + 1, diag1)
            for t, tile in enumerate((one, two)):
                row, col = (2, t) if c == 0 else (t, 3)
                put(j, row, col, tile)
                put(j, col, row, tile.T)


def square(core, mine, oth):
    size = mine.shape[1]
    return pl.pallas_call(
        square_kernel,
        grid_spec=pltpu.PrefetchScalarGridSpec(
            num_scalar_prefetch=1, grid=(), in_specs=in_vmem(2), out_specs=pl.BlockSpec(memory_space=pltpu.VMEM)
        ),
        out_shape=jax.ShapeDtypeStruct((2, 4 * size, 4 * size), F32),
        compiler_params=params(),
        cost_estimate=pl.CostEstimate(flops=0, bytes_accessed=4 * MIB, transcendentals=0),
        name="square",
    )(core, mine, oth)


def order_kernel(chip, *refs):
    h = refs[0].shape[0]
    for bits, ref in enumerate(refs[:-1]):
        refs[-1][pl.ds(pl.multiple_of((chip[0] ^ bits) * h, 8), h)] = ref[...]


def order(chip, came):
    h, width = came[0].shape
    return pl.pallas_call(
        order_kernel,
        grid_spec=pltpu.PrefetchScalarGridSpec(
            num_scalar_prefetch=1, grid=(), in_specs=in_vmem(len(came)), out_specs=pl.BlockSpec(memory_space=pltpu.VMEM)
        ),
        out_shape=jax.ShapeDtypeStruct((len(came) * h, width), F32),
        compiler_params=params(),
        cost_estimate=pl.CostEstimate(flops=0, bytes_accessed=2 * MIB, transcendentals=0),
        name="order",
    )(chip, *came)


def place_kernel(wanted, core, y0, y1, z0, z1, oth, out):
    _, rows, _, half = y0.shape
    part = out.shape[1]
    for step in range(2 * rows // part):

        @pl.when(pl.program_id(0) == step)
        def _():
            j = step * part // rows
            which, at = PLACES[j][0]
            for q in range(step * part % rows, step * part % rows + part):
                keep = wanted[j * rows + q] != 0
                mine = jnp.where(keep, -((y0, y1)[which][at, q] + (z0, z1)[which][at, q]), 0.0)
                other = jnp.where(keep, -oth[j, q], 0.0)
                out[0, q % part, :, :half] = jnp.where(core[0] == 0, mine, other)
                out[0, q % part, :, half:] = jnp.where(core[0] == 0, other, mine)


def place(wanted, core, ys, recv, oth):
    _, rows, size, half = ys[0].shape
    return pl.pallas_call(
        place_kernel,
        grid_spec=pltpu.PrefetchScalarGridSpec(
            num_scalar_prefetch=2,
            grid=(4,),
            in_specs=in_vmem(5),
            out_specs=pl.BlockSpec((1, rows // 2, size, 2 * half), lambda i, *_: (i // 2, i % 2, 0, 0)),
        ),
        out_shape=jax.ShapeDtypeStruct((2, rows, size, 2 * half), F32),
        compiler_params=params(),
        cost_estimate=pl.CostEstimate(flops=0, bytes_accessed=5 * MIB, transcendentals=0),
        name="place",
    )(wanted, core, *ys, *recv, oth)


def any_mesh(sigma_anc, panel, pattern, linv):
    high = lax.Precision.HIGH
    einsum = functools.partial(jnp.einsum, precision=high, preferred_element_type=F32)
    rows, cols = lax.axis_size("row"), lax.axis_size("col")
    row_ids = jnp.arange(sigma_anc.shape[0], dtype=jnp.int32) * rows + lax.axis_index("row")
    col_ids = jnp.arange(sigma_anc.shape[1], dtype=jnp.int32) * cols + lax.axis_index("col")
    wanted = jnp.any(pattern[:, :, None] == row_ids, axis=1).astype(F32)[:, :, None, None]
    u = einsum("sqiw,swv->sqiv", panel, linv) * wanted
    pick = (col_ids[:, None] == row_ids[None, :]).astype(F32)
    u_cols = lax.psum(jnp.einsum("kq,sqiw->skiw", pick, u, precision=lax.Precision.HIGHEST), "row")
    y = lax.psum(einsum("qkij,skjw->sqiw", sigma_anc, u_cols), "col") * wanted
    total = lax.psum(einsum("sqiw,sqiv->swv", u, y), "row")
    return -y, einsum("siw,siv->swv", linv, linv) + total


def ring_place(chip, chips):
    z, x = chip // 2, chip % 2
    return jnp.where(x == 0, z, chips - 1 - z)


def ring_chip(place, chips):
    place = place % chips
    return jnp.where(place < chips // 2, 2 * place, 2 * (chips - 1 - place) + 1)


def pair_rows(sigma_anc, panel, linv, wanted):
    supers, rows, size, width = panel.shape
    half = width // 2
    n_row = lax.axis_size("row")
    chips = n_row // 2
    me, plane = lax.axis_index("row"), lax.axis_index("col")
    chip, core = me // 2, me % 2
    place_here = ring_place(chip, chips)
    across = [(i, i ^ 1) for i in range(n_row)]
    pair = [(0, 1), (1, 0)]
    order = [2 * q for q in range(chips // 2)] + [2 * (chips - 1 - q) + 1 for q in range(chips // 2, chips)]
    around = []
    for q in range(chips):
        around.append((2 * order[q], 2 * order[(q + 1) % chips]))
        around.append((2 * order[q] + 1, 2 * order[(q - 1) % chips] + 1))

    near, away = update(core[None], far(panel), far(linv))
    away_oth = lax.ppermute(away, "row", across)
    first = jnp.where(core == plane, near, away_oth)
    wanted_here = jnp.where(plane == 0, wanted[0], wanted[1]).reshape(-1)
    wanted_rows = jnp.where(core == 0, wanted, wanted[::-1])
    wanted_rows = lax.dynamic_index_in_dim(wanted_rows, chip, 1, keepdims=False).reshape(-1)
    held = [first[:rows], first[rows:]]
    accs = [jnp.zeros((count, rows, size, half), F32) for count in (2, 2)]
    span = width // (2 * chips)
    share = lax.dynamic_slice_in_dim(linv, (chip * 2 + plane) * span, span, axis=1)
    waiting = []
    s_own = far(sigma_anc)
    s_oth = near_oth = None
    for step in range(chips):
        origin = ring_chip(place_here + jnp.where(core == 0, -step, step), chips)
        blocks = tuple(held)
        if step < chips - 1:
            held[0] = lax.ppermute(held[0], "row", around)
            while len(waiting) > (step < chips // 2):
                accs = add_columns(*waiting.pop(0), accs)
            if step == 2:
                wanted_rows, share, held[1] = lax.optimization_barrier((wanted_rows, share, held[1]))
            sent, *accs = lax.optimization_barrier((held[1], *accs))
            held[1] = lax.ppermute(sent, "row", around)
        if s_oth is None:
            u_kept = [far(near), far(away)]
            s_sent, near_sent, _ = lax.optimization_barrier((sigma_anc, near, away_oth))
            s_oth = lax.ppermute(s_sent, "row", across)
            near_oth = lax.ppermute(near_sent, "row", across)
        waiting.append((wanted_here, origin[None], *blocks, s_own, s_oth))
    for last in waiting:
        accs = add_columns(*last, accs)

    part = inner(wanted_rows, core[None], *u_kept, away_oth, near_oth, share, accs)
    total, recv = all_sum(part, accs, chip, chips, pair)
    y_oth = lax.ppermute(accs[0] + recv[0], "row", across)
    total_oth = lax.ppermute(total, "row", across)
    sigma_sj = place(wanted_rows[:ITEMS], core[None], accs, recv, y_oth)
    return sigma_sj, square(core[None], total, total_oth)


def all_sum(x, ys, chip, chips, pair):
    shape = x.shape
    flat = x.reshape(-1, shape[-1])
    h = flat.shape[0] // chips

    def flip(bits):
        return [(i, i ^ (2 * bits)) for i in range(2 * chips)]

    most = lax.ppermute(ys[0], "col", pair)
    mine = lax.dynamic_slice_in_dim(flat, chip * h, h)
    for bits in range(1, chips):
        sent = lax.dynamic_slice_in_dim(flat, (chip ^ bits) * h, h)
        mine = mine + lax.ppermute(sent, "row", flip(bits))
    mine, most = lax.optimization_barrier((mine, most))
    mine = mine + lax.ppermute(mine, "col", pair)
    mine, sent = lax.optimization_barrier((mine, ys[1]))
    rest = lax.ppermute(sent, "col", pair)
    came = [mine] + [lax.ppermute(mine, "row", flip(bits)) for bits in range(1, chips)]
    *came, rest = lax.optimization_barrier((*came, rest))
    return order(chip[None], came).reshape(shape), (most, rest)


def local(sigma_anc, panel, pattern, linv):
    n_row, n_col = lax.axis_size("row"), lax.axis_size("col")
    rows = sigma_anc.shape[0]
    supers = panel.shape[0]
    if (n_row, n_col, rows * supers) != (16, 2, ITEMS):
        return any_mesh(sigma_anc, panel, pattern, linv)
    chips = n_row // 2
    e = jnp.arange(ITEMS, dtype=jnp.int32)
    ids = (
        (e % rows)[None, None, :] * n_row
        + 2 * jnp.arange(chips, dtype=jnp.int32)[None, :, None]
        + jnp.arange(2, dtype=jnp.int32)[:, None, None]
    )
    hit = jnp.any(pattern[:, None, None, None, :] == ids[None, ..., None], axis=-1)
    wanted = jnp.where(e // rows == 0, hit[0], hit[1])
    return pair_rows(sigma_anc, panel, linv, wanted.astype(jnp.int32))


def solution(mesh):
    return jax.shard_map(
        local,
        mesh=mesh,
        in_specs=(P("row", "col", None, None), P(None, "row", None, None), P(), P()),
        out_specs=(P(None, "row", None, None), P()),
        check_vma=False,
    )
```

```python
import functools

import jax
import jax.numpy as jnp
from jax import lax
from jax.experimental import pallas as pl
from jax.experimental.pallas import tpu as pltpu
from jax.sharding import PartitionSpec as P

F32 = jnp.float32
BF16 = jnp.bfloat16
MIB = 1 << 20


def split(x):
    hi = x.astype(BF16)
    return hi, (x - hi.astype(F32)).astype(BF16)


def dot3(a, b, a_axis=1, b_axis=0):
    left = jnp.concatenate([a[0], a[1], a[0]], axis=a_axis)
    right = jnp.concatenate([b[0], b[0], b[1]], axis=b_axis)
    dims = (((a_axis,), (b_axis,)), ((), ()))
    return lax.dot_general(left, right, dims, preferred_element_type=F32)


def three(a, b):
    dot = functools.partial(jnp.dot, preferred_element_type=F32)
    return dot(a[0], b[0]) + (dot(a[0], b[1]) + dot(a[1], b[0]))


ITEMS = 8
FIRST = 9


def where_is(j, source, q, rows):
    n = (1 - source) * 2 * rows + j * rows + q
    return (0, n) if n < FIRST else (1, n - FIRST)


def in_vmem(count):
    return [pl.BlockSpec(memory_space=pltpu.VMEM)] * count


def far(x):
    return pltpu.with_memory_space_constraint(x, pltpu.HBM)


def params(mib=24):
    return pltpu.CompilerParams(vmem_limit_bytes=mib * MIB)


def update_kernel(core, panel, linv, near, away, rows_in, low_in, arrived):
    supers, rows, size, width = panel.shape
    half = width // 2
    swapped = core[0] == 1

    def copies(j):
        yield pltpu.make_async_copy(linv.at[j], low_in.at[j], arrived.at[j, rows])
        for q in range(rows):
            yield pltpu.make_async_copy(panel.at[j, q], rows_in.at[j, q], arrived.at[j, q])

    for j in range(supers):
        for copy in copies(j):
            copy.start()
    for j in range(supers):
        for copy in copies(j):
            copy.wait()
        left = split(rows_in[j].reshape(rows * size, width))
        first = three(left, split(low_in[j, :, :half]))
        second = three([x[:, half:] for x in left], split(low_in[j, half:, half:]))
        here, there = jnp.where(swapped, second, first), jnp.where(swapped, first, second)
        near[j * rows:(j + 1) * rows] = here.reshape(rows, size, half)
        away[j * rows:(j + 1) * rows] = there.reshape(rows, size, half)


def update(core, panel, linv):
    supers, rows, size, width = panel.shape
    hbm = pl.BlockSpec(memory_space=pltpu.HBM)
    return pl.pallas_call(
        update_kernel,
        grid_spec=pltpu.PrefetchScalarGridSpec(
            num_scalar_prefetch=1,
            grid=(),
            in_specs=[hbm, hbm],
            out_specs=in_vmem(2),
            scratch_shapes=[
                pltpu.VMEM(panel.shape, F32),
                pltpu.VMEM(linv.shape, F32),
                pltpu.SemaphoreType.DMA((supers, rows + 1)),
            ],
        ),
        out_shape=[jax.ShapeDtypeStruct((ITEMS, size, width // 2), F32)] * 2,
        compiler_params=params(32),
        cost_estimate=pl.CostEstimate(
            flops=6 * supers * rows * size * width * width, bytes_accessed=6 * MIB, transcendentals=0
        ),
        name="update",
    )(core, panel, linv)


def column_kernel(wanted, chip, u0, u1, own, oth, *refs):
    accs, outs, (blocks, arrived) = refs[:2], refs[2:4], refs[4:]
    rows, cols, size, _ = own.shape
    items, _, width = u0.shape

    def copy(i, source):
        ref = (own, oth)[source]
        column = i * (cols // items) + chip[0]
        return pltpu.make_async_copy(ref.at[:, column], blocks.at[i, source], arrived.at[i, source])

    def wants(i):
        at = chip[0] * ITEMS + i
        return wanted[at] != 0, wanted[at + items] != 0

    for i in range(items):
        first, second = wants(i)

        @pl.when(first | second)
        def _():
            copy(i, 0).start()
            copy(i, 1).start()

    for acc, out in zip(accs, outs):
        out[...] = acc[...]

    def body(i, carry):
        first, second = wants(i)

        @pl.when(first | second)
        def _():
            pair = [jnp.where(first, u0[i], 0.0), jnp.where(second, u1[i], 0.0)]
            right = split(jnp.concatenate(pair, axis=1))
            copy(i, 0).wait()
            copy(i, 1).wait()
            left = split(blocks[i].reshape(2 * rows * size, size))
            product = dot3(left, right).reshape(2, rows, size, 2 * width)
            for j in range(2):
                for source in range(2):
                    for q in range(rows):
                        which, at = where_is(j, source, q, rows)
                        outs[which][at] += product[source, q, :, j * width:(j + 1) * width]

        return carry

    lax.fori_loop(0, items, body, 0)


def add_columns(wanted, chip, u0, u1, own, oth, accs):
    items, size, width = u0.shape
    rows = own.shape[0]
    hbm = pl.BlockSpec(memory_space=pltpu.HBM)
    return pl.pallas_call(
        column_kernel,
        grid_spec=pltpu.PrefetchScalarGridSpec(
            num_scalar_prefetch=2,
            grid=(),
            in_specs=in_vmem(2) + [hbm, hbm] + in_vmem(2),
            out_specs=in_vmem(2),
            scratch_shapes=[
                pltpu.VMEM((items, 2, rows, size, size), F32),
                pltpu.SemaphoreType.DMA((items, 2)),
            ],
        ),
        out_shape=[jax.ShapeDtypeStruct(acc.shape, F32) for acc in accs],
        input_output_aliases={6 + i: i for i in range(2)},
        compiler_params=params(24),
        cost_estimate=pl.CostEstimate(
            flops=24 * items * rows * size * size * width, bytes_accessed=6 * MIB, transcendentals=0
        ),
        name="add_columns",
    )(wanted, chip, u0, u1, own, oth, *accs)


def inner_kernel(wanted, core, near, away, near_oth, away_oth, share, y0, y1, out, held, arrived):
    _, size, half = y0.shape
    rows = ITEMS // 2
    copies = [
        pltpu.make_async_copy(ref, held.at[k], arrived.at[k])
        for k, ref in enumerate((near, near_oth, away, away_oth))
    ]
    for copy in copies:
        copy.start()

    def stack(j, k, start, begin, end):
        parts = [held[k + s, j * rows:(j + 1) * rows, :, begin:end].reshape(rows * size, end - begin) for s in range(2)]
        return split(jnp.concatenate(parts + [start[:, begin:end]], axis=0))

    for j in range(2):
        low, high = share[j, :, :half], share[j, :, half:]
        here, there = jnp.where(core[0] == 1, high, low), jnp.where(core[0] == 1, low, high)
        right = []
        for source in range(2):
            for q in range(rows):
                which, at = where_is(j, source, q, rows)
                y = (y0, y1)[which][at]
                right.append(jnp.where(wanted[source * ITEMS + j * rows + q] != 0, y, 0.0))
        right = split(jnp.concatenate(right + [here], axis=0))
        first = 5 * j
        if j == 0:
            copies[0].wait()
            copies[1].wait()
        diag = dot3(stack(j, 0, here, 0, half), right, 0, 0)
        out[first] = diag[:size, :size]
        out[first + 1] = diag[size:, :size]
        out[first + 2] = diag[size:, size:]
        if j == 0:
            copies[2].wait()
            copies[3].wait()

        @pl.when(core[0] == 0)
        def _():
            cross = dot3(stack(j, 2, there, 0, size), right, 0, 0)
            out[first + 3] = cross[:, :size]
            out[first + 4] = cross[:, size:]

        @pl.when(core[0] != 0)
        def _():
            cross = dot3(stack(j, 2, there, 0, half), [x[:, size:] for x in right], 0, 0)
            out[first + 3] = cross[:size]
            out[first + 4] = cross[size:]


def inner(wanted, core, near, away, near_oth, away_oth, share, ys):
    _, size, half = ys[0].shape
    hbm = pl.BlockSpec(memory_space=pltpu.HBM)
    return pl.pallas_call(
        inner_kernel,
        grid_spec=pltpu.PrefetchScalarGridSpec(
            num_scalar_prefetch=2,
            grid=(),
            in_specs=[hbm] * 4 + in_vmem(3),
            out_specs=pl.BlockSpec(memory_space=pltpu.VMEM),
            scratch_shapes=[pltpu.VMEM((4, *near.shape), F32), pltpu.SemaphoreType.DMA((4,))],
        ),
        out_shape=jax.ShapeDtypeStruct((10, size, size), F32),
        compiler_params=params(36),
        cost_estimate=pl.CostEstimate(
            flops=18 * ITEMS * size * half * half, bytes_accessed=8 * MIB, transcendentals=0
        ),
        name="inner",
    )(wanted, core, near, away, near_oth, away_oth, share, *ys)


def square_kernel(core, mine, oth, out):
    size = mine.shape[1]

    def put(j, row, col, tile):
        out[j, row * size:(row + 1) * size, col * size:(col + 1) * size] = tile

    for j in range(2):
        for c in range(2):
            diag0, below, diag1, one, two = (jnp.where(core[0] == c, mine[5 * j + k], oth[5 * j + k]) for k in range(5))
            put(j, 2 * c, 2 * c, diag0)
            put(j, 2 * c + 1, 2 * c, below)
            put(j, 2 * c, 2 * c + 1, below.T)
            put(j, 2 * c + 1, 2 * c + 1, diag1)
            for t, tile in enumerate((one, two)):
                row, col = (2, t) if c == 0 else (t, 3)
                put(j, row, col, tile)
                put(j, col, row, tile.T)


def square(core, mine, oth):
    size = mine.shape[1]
    return pl.pallas_call(
        square_kernel,
        grid_spec=pltpu.PrefetchScalarGridSpec(
            num_scalar_prefetch=1, grid=(), in_specs=in_vmem(2), out_specs=pl.BlockSpec(memory_space=pltpu.VMEM)
        ),
        out_shape=jax.ShapeDtypeStruct((2, 4 * size, 4 * size), F32),
        compiler_params=params(),
        cost_estimate=pl.CostEstimate(flops=0, bytes_accessed=4 * MIB, transcendentals=0),
        name="square",
    )(core, mine, oth)


def order_kernel(chip, *refs):
    h = refs[0].shape[0]
    for bits, ref in enumerate(refs[:-1]):
        refs[-1][pl.ds(pl.multiple_of((chip[0] ^ bits) * h, 8), h)] = ref[...]


def order(chip, came):
    h, width = came[0].shape
    return pl.pallas_call(
        order_kernel,
        grid_spec=pltpu.PrefetchScalarGridSpec(
            num_scalar_prefetch=1, grid=(), in_specs=in_vmem(len(came)), out_specs=pl.BlockSpec(memory_space=pltpu.VMEM)
        ),
        out_shape=jax.ShapeDtypeStruct((len(came) * h, width), F32),
        compiler_params=params(),
        cost_estimate=pl.CostEstimate(flops=0, bytes_accessed=2 * MIB, transcendentals=0),
        name="order",
    )(chip, *came)


def place_kernel(wanted, core, y0, y1, z0, z1, oth, out):
    rows, half = ITEMS // 2, y0.shape[2]
    part = out.shape[1]
    for step in range(2 * rows // part):

        @pl.when(pl.program_id(0) == step)
        def _():
            j = step * part // rows
            for q in range(step * part % rows, step * part % rows + part):
                keep = wanted[j * rows + q] != 0
                which, at = where_is(j, 0, q, rows)
                mine = jnp.where(keep, -((y0, y1)[which][at] + (z0, z1)[which][at]), 0.0)
                other = jnp.where(keep, -oth[j * rows + q], 0.0)
                out[0, q % part, :, :half] = jnp.where(core[0] == 0, mine, other)
                out[0, q % part, :, half:] = jnp.where(core[0] == 0, other, mine)


def place(wanted, core, ys, recv, oth):
    _, size, half = ys[0].shape
    rows = ITEMS // 2
    return pl.pallas_call(
        place_kernel,
        grid_spec=pltpu.PrefetchScalarGridSpec(
            num_scalar_prefetch=2,
            grid=(4,),
            in_specs=in_vmem(5),
            out_specs=pl.BlockSpec((1, rows // 2, size, 2 * half), lambda i, *_: (i // 2, i % 2, 0, 0)),
        ),
        out_shape=jax.ShapeDtypeStruct((2, rows, size, 2 * half), F32),
        compiler_params=params(),
        cost_estimate=pl.CostEstimate(flops=0, bytes_accessed=5 * MIB, transcendentals=0),
        name="place",
    )(wanted, core, *ys, *recv, oth)


def any_mesh(sigma_anc, panel, pattern, linv):
    high = lax.Precision.HIGH
    einsum = functools.partial(jnp.einsum, precision=high, preferred_element_type=F32)
    rows, cols = lax.axis_size("row"), lax.axis_size("col")
    row_ids = jnp.arange(sigma_anc.shape[0], dtype=jnp.int32) * rows + lax.axis_index("row")
    col_ids = jnp.arange(sigma_anc.shape[1], dtype=jnp.int32) * cols + lax.axis_index("col")
    wanted = jnp.any(pattern[:, :, None] == row_ids, axis=1).astype(F32)[:, :, None, None]
    u = einsum("sqiw,swv->sqiv", panel, linv) * wanted
    pick = (col_ids[:, None] == row_ids[None, :]).astype(F32)
    u_cols = lax.psum(jnp.einsum("kq,sqiw->skiw", pick, u, precision=lax.Precision.HIGHEST), "row")
    y = lax.psum(einsum("qkij,skjw->sqiw", sigma_anc, u_cols), "col") * wanted
    total = lax.psum(einsum("sqiw,sqiv->swv", u, y), "row")
    return -y, einsum("siw,siv->swv", linv, linv) + total


def ring_place(chip, chips):
    z, x = chip // 2, chip % 2
    return jnp.where(x == 0, z, chips - 1 - z)


def ring_chip(place, chips):
    place = place % chips
    return jnp.where(place < chips // 2, 2 * place, 2 * (chips - 1 - place) + 1)


def pair_rows(sigma_anc, panel, linv, wanted):
    supers, rows, size, width = panel.shape
    half = width // 2
    n_row = lax.axis_size("row")
    chips = n_row // 2
    me, plane = lax.axis_index("row"), lax.axis_index("col")
    chip, core = me // 2, me % 2
    place_here = ring_place(chip, chips)
    across = [(i, i ^ 1) for i in range(n_row)]
    pair = [(0, 1), (1, 0)]
    order = [2 * q for q in range(chips // 2)] + [2 * (chips - 1 - q) + 1 for q in range(chips // 2, chips)]
    around = []
    for q in range(chips):
        around.append((2 * order[q], 2 * order[(q + 1) % chips]))
        around.append((2 * order[q] + 1, 2 * order[(q - 1) % chips] + 1))

    near, away = update(core[None], far(panel), far(linv))
    away_oth = lax.ppermute(away, "row", across)
    first = jnp.where(core == plane, near, away_oth)
    wanted_here = jnp.where(plane == 0, wanted[0], wanted[1]).reshape(-1)
    wanted_rows = jnp.where(core == 0, wanted, wanted[::-1])
    wanted_rows = lax.dynamic_index_in_dim(wanted_rows, chip, 1, keepdims=False).reshape(-1)
    held = [first[:rows], first[rows:]]
    accs = [jnp.zeros((count, size, half), F32) for count in (FIRST, 2 * ITEMS - FIRST)]
    span = width // (2 * chips)
    share = lax.dynamic_slice_in_dim(linv, (chip * 2 + plane) * span, span, axis=1)
    waiting = []
    s_own = far(sigma_anc)
    s_oth = near_oth = None
    for step in range(chips):
        origin = ring_chip(place_here + jnp.where(core == 0, -step, step), chips)
        blocks = tuple(held)
        if step < chips - 1:
            held[0] = lax.ppermute(held[0], "row", around)
            while len(waiting) > 1:
                accs = add_columns(*waiting.pop(0), accs)
            if step == 3:
                us = [far(u) for u in us]
                wanted_rows, share, held[1], *us = lax.optimization_barrier((wanted_rows, share, held[1], *us))
            sent, *accs = lax.optimization_barrier((held[1], *accs))
            held[1] = lax.ppermute(sent, "row", around)
        if s_oth is None:
            s_sent, near_sent, _ = lax.optimization_barrier((sigma_anc, near, away_oth))
            s_oth = lax.ppermute(s_sent, "row", across)
            near_oth = lax.ppermute(near_sent, "row", across)
            us = [near, away, away_oth, near_oth]
        waiting.append((wanted_here, origin[None], *blocks, s_own, s_oth))
    for last in waiting:
        accs = add_columns(*last, accs)

    part = inner(wanted_rows, core[None], *us, share, accs)
    total, recv, y_oth = all_sum(part, accs, chip, chips, pair, across)
    total_oth = lax.ppermute(total, "row", across)
    sigma_sj = place(wanted_rows[:ITEMS], core[None], accs, recv, y_oth)
    return sigma_sj, square(core[None], total, total_oth)


def all_sum(x, ys, chip, chips, pair, across):
    shape = x.shape
    flat = x.reshape(-1, shape[-1])
    h = flat.shape[0] // chips

    def flip(bits):
        return [(i, i ^ (2 * bits)) for i in range(2 * chips)]

    most = lax.ppermute(ys[0], "col", pair)
    mine = lax.dynamic_slice_in_dim(flat, chip * h, h)
    for bits in range(1, chips):
        sent = lax.dynamic_slice_in_dim(flat, (chip ^ bits) * h, h)
        mine = mine + lax.ppermute(sent, "row", flip(bits))
    mine, most = lax.optimization_barrier((mine, most))
    mine = mine + lax.ppermute(mine, "col", pair)
    y_oth = lax.ppermute(ys[0][:ITEMS] + most[:ITEMS], "row", across)
    mine, sent, y_oth = lax.optimization_barrier((mine, ys[1], y_oth))
    rest = lax.ppermute(sent, "col", pair)
    came = [mine] + [lax.ppermute(mine, "row", flip(bits)) for bits in range(1, chips)]
    *came, rest = lax.optimization_barrier((*came, rest))
    return order(chip[None], came).reshape(shape), (most, rest), y_oth


def local(sigma_anc, panel, pattern, linv):
    n_row, n_col = lax.axis_size("row"), lax.axis_size("col")
    rows = sigma_anc.shape[0]
    supers = panel.shape[0]
    if (n_row, n_col, rows * supers) != (16, 2, ITEMS):
        return any_mesh(sigma_anc, panel, pattern, linv)
    chips = n_row // 2
    e = jnp.arange(ITEMS, dtype=jnp.int32)
    ids = (
        (e % rows)[None, None, :] * n_row
        + 2 * jnp.arange(chips, dtype=jnp.int32)[None, :, None]
        + jnp.arange(2, dtype=jnp.int32)[:, None, None]
    )
    hit = jnp.any(pattern[:, None, None, None, :] == ids[None, ..., None], axis=-1)
    wanted = jnp.where(e // rows == 0, hit[0], hit[1])
    return pair_rows(sigma_anc, panel, linv, wanted.astype(jnp.int32))


def solution(mesh):
    return jax.shard_map(
        local,
        mesh=mesh,
        in_specs=(P("row", "col", None, None), P(None, "row", None, None), P(), P()),
        out_specs=(P(None, "row", None, None), P()),
        check_vma=False,
    )
```

```python
import functools

import jax
import jax.numpy as jnp
from jax import lax
from jax.experimental import pallas as pl
from jax.experimental.pallas import tpu as pltpu
from jax.sharding import PartitionSpec as P

F32 = jnp.float32
BF16 = jnp.bfloat16
MIB = 1 << 20


def split(x):
    hi = x.astype(BF16)
    return hi, (x - hi.astype(F32)).astype(BF16)


def dot3(a, b, a_axis=1, b_axis=0):
    left = jnp.concatenate([a[0], a[1], a[0]], axis=a_axis)
    right = jnp.concatenate([b[0], b[0], b[1]], axis=b_axis)
    dims = (((a_axis,), (b_axis,)), ((), ()))
    return lax.dot_general(left, right, dims, preferred_element_type=F32)


def three(a, b):
    dot = functools.partial(jnp.dot, preferred_element_type=F32)
    return dot(a[0], b[0]) + (dot(a[0], b[1]) + dot(a[1], b[0]))


ITEMS = 8
FIRST = 9


def where_is(j, source, q, rows):
    n = (1 - source) * 2 * rows + j * rows + q
    return (0, n) if n < FIRST else (1, n - FIRST)


def in_vmem(count):
    return [pl.BlockSpec(memory_space=pltpu.VMEM)] * count


def far(x):
    return pltpu.with_memory_space_constraint(x, pltpu.HBM)


def params(mib=24):
    return pltpu.CompilerParams(vmem_limit_bytes=mib * MIB)


def update_kernel(core, panel, linv, near, away, rows_in, low_in, arrived):
    supers, rows, size, width = panel.shape
    half = width // 2
    swapped = core[0] == 1

    def copies(j):
        yield pltpu.make_async_copy(linv.at[j], low_in.at[j], arrived.at[j, rows])
        for q in range(rows):
            yield pltpu.make_async_copy(panel.at[j, q], rows_in.at[j, q], arrived.at[j, q])

    for j in range(supers):
        for copy in copies(j):
            copy.start()
    for j in range(supers):
        for copy in copies(j):
            copy.wait()
        left = split(rows_in[j].reshape(rows * size, width))
        first = three(left, split(low_in[j, :, :half]))
        second = three([x[:, half:] for x in left], split(low_in[j, half:, half:]))
        here, there = jnp.where(swapped, second, first), jnp.where(swapped, first, second)
        near[j * rows:(j + 1) * rows] = here.reshape(rows, size, half)
        away[j * rows:(j + 1) * rows] = there.reshape(rows, size, half)


def update(core, panel, linv):
    supers, rows, size, width = panel.shape
    hbm = pl.BlockSpec(memory_space=pltpu.HBM)
    return pl.pallas_call(
        update_kernel,
        grid_spec=pltpu.PrefetchScalarGridSpec(
            num_scalar_prefetch=1,
            grid=(),
            in_specs=[hbm, hbm],
            out_specs=in_vmem(2),
            scratch_shapes=[
                pltpu.VMEM(panel.shape, F32),
                pltpu.VMEM(linv.shape, F32),
                pltpu.SemaphoreType.DMA((supers, rows + 1)),
            ],
        ),
        out_shape=[jax.ShapeDtypeStruct((ITEMS, size, width // 2), F32)] * 2,
        compiler_params=params(32),
        cost_estimate=pl.CostEstimate(
            flops=6 * supers * rows * size * width * width, bytes_accessed=6 * MIB, transcendentals=0
        ),
        name="update",
    )(core, panel, linv)


def column_kernel(wanted, chip, u0, u1, own, oth, *refs):
    accs, outs, (blocks, arrived) = refs[:2], refs[2:4], refs[4:]
    rows, cols, size, _ = own.shape
    items, _, width = u0.shape

    def copy(i, source):
        ref = (own, oth)[source]
        column = i * (cols // items) + chip[0]
        return pltpu.make_async_copy(ref.at[:, column], blocks.at[i, source], arrived.at[i, source])

    def wants(i):
        at = chip[0] * ITEMS + i
        return wanted[at] != 0, wanted[at + items] != 0

    for i in range(items):
        first, second = wants(i)

        @pl.when(first | second)
        def _():
            copy(i, 0).start()
            copy(i, 1).start()

    for acc, out in zip(accs, outs):
        out[...] = acc[...]

    def body(i, carry):
        first, second = wants(i)

        @pl.when(first | second)
        def _():
            pair = [jnp.where(first, u0[i], 0.0), jnp.where(second, u1[i], 0.0)]
            right = split(jnp.concatenate(pair, axis=1))
            copy(i, 0).wait()
            copy(i, 1).wait()
            left = split(blocks[i].reshape(2 * rows * size, size))
            product = dot3(left, right).reshape(2, rows, size, 2 * width)
            for j in range(2):
                for source in range(2):
                    for q in range(rows):
                        which, at = where_is(j, source, q, rows)
                        outs[which][at] += product[source, q, :, j * width:(j + 1) * width]

        return carry

    lax.fori_loop(0, items, body, 0)


def add_columns(wanted, chip, u0, u1, own, oth, accs):
    items, size, width = u0.shape
    rows = own.shape[0]
    hbm = pl.BlockSpec(memory_space=pltpu.HBM)
    return pl.pallas_call(
        column_kernel,
        grid_spec=pltpu.PrefetchScalarGridSpec(
            num_scalar_prefetch=2,
            grid=(),
            in_specs=in_vmem(2) + [hbm, hbm] + in_vmem(2),
            out_specs=in_vmem(2),
            scratch_shapes=[
                pltpu.VMEM((items, 2, rows, size, size), F32),
                pltpu.SemaphoreType.DMA((items, 2)),
            ],
        ),
        out_shape=[jax.ShapeDtypeStruct(acc.shape, F32) for acc in accs],
        input_output_aliases={6 + i: i for i in range(2)},
        compiler_params=params(24),
        cost_estimate=pl.CostEstimate(
            flops=24 * items * rows * size * size * width, bytes_accessed=6 * MIB, transcendentals=0
        ),
        name="add_columns",
    )(wanted, chip, u0, u1, own, oth, *accs)


def inner_kernel(wanted, here_is, *refs):
    us, (share, y0, y1), outs, (held, tiles, arrived) = refs[:4], refs[4:7], refs[7:15], refs[15:]
    _, size, half = y0.shape
    rows = ITEMS // 2
    core = here_is

    def each(k, j, task):
        for q in range(rows):
            e = j * rows + q
            for source in range(2):

                @pl.when(wanted[source * ITEMS + e] != 0)
                def _():
                    task(pltpu.make_async_copy(us[k + source].at[e], held.at[k + source, e], arrived.at[k + source, e]))

    for j in range(2):
        for k in (0, 2):
            each(k, j, lambda copy: copy.start())

    def stack(j, k, start, begin, end):
        parts = [
            jnp.where(wanted[s * ITEMS + j * rows + q] != 0, held[k + s, j * rows + q, :, begin:end], 0.0)
            for s in range(2)
            for q in range(rows)
        ]
        return split(jnp.concatenate(parts + [start[:, begin:end]], axis=0))

    def put(k, tile):
        tiles[k * size:(k + 1) * size] = tile

    for j in range(2):
        low, high = share[j, :, :half], share[j, :, half:]
        here, there = jnp.where(core[0] == 1, high, low), jnp.where(core[0] == 1, low, high)
        right = []
        for source in range(2):
            for q in range(rows):
                which, at = where_is(j, source, q, rows)
                y = (y0, y1)[which][at]
                right.append(jnp.where(wanted[source * ITEMS + j * rows + q] != 0, y, 0.0))
        right = split(jnp.concatenate(right + [here], axis=0))
        first = 5 * j
        each(0, j, lambda copy: copy.wait())
        diag = dot3(stack(j, 0, here, 0, half), right, 0, 0)
        put(first, diag[:size, :size])
        put(first + 1, diag[size:, :size])
        put(first + 2, diag[size:, size:])
        each(2, j, lambda copy: copy.wait())

        @pl.when(core[0] == 0)
        def _():
            cross = dot3(stack(j, 2, there, 0, size), right, 0, 0)
            put(first + 3, cross[:, :size])
            put(first + 4, cross[:, size:])

        @pl.when(core[0] != 0)
        def _():
            cross = dot3(stack(j, 2, there, 0, half), [x[:, size:] for x in right], 0, 0)
            put(first + 3, cross[:size])
            put(first + 4, cross[size:])

    h = outs[0].shape[0]
    for bits, out in enumerate(outs):
        out[...] = tiles[pl.ds(pl.multiple_of((here_is[1] ^ bits) * h, 8), h)]


def inner(wanted, here_is, us, share, ys, chips):
    _, size, half = ys[0].shape
    hbm = pl.BlockSpec(memory_space=pltpu.HBM)
    return pl.pallas_call(
        inner_kernel,
        grid_spec=pltpu.PrefetchScalarGridSpec(
            num_scalar_prefetch=2,
            grid=(),
            in_specs=[hbm] * 4 + in_vmem(3),
            out_specs=in_vmem(chips),
            scratch_shapes=[
                pltpu.VMEM((4, *us[0].shape), F32),
                pltpu.VMEM((10 * size, size), F32),
                pltpu.SemaphoreType.DMA((4, ITEMS)),
            ],
        ),
        out_shape=[jax.ShapeDtypeStruct((10 * size // chips, size), F32)] * chips,
        compiler_params=params(36),
        cost_estimate=pl.CostEstimate(
            flops=18 * ITEMS * size * half * half, bytes_accessed=8 * MIB, transcendentals=0
        ),
        name="inner",
    )(wanted, here_is, *us, share, *ys)


def square_kernel(core, mine, oth, out):
    size = mine.shape[1]

    def put(j, row, col, tile):
        out[j, row * size:(row + 1) * size, col * size:(col + 1) * size] = tile

    for j in range(2):
        for c in range(2):
            diag0, below, diag1, one, two = (jnp.where(core[0] == c, mine[5 * j + k], oth[5 * j + k]) for k in range(5))
            put(j, 2 * c, 2 * c, diag0)
            put(j, 2 * c + 1, 2 * c, below)
            put(j, 2 * c, 2 * c + 1, below.T)
            put(j, 2 * c + 1, 2 * c + 1, diag1)
            for t, tile in enumerate((one, two)):
                row, col = (2, t) if c == 0 else (t, 3)
                put(j, row, col, tile)
                put(j, col, row, tile.T)


def square(core, mine, oth):
    size = mine.shape[1]
    return pl.pallas_call(
        square_kernel,
        grid_spec=pltpu.PrefetchScalarGridSpec(
            num_scalar_prefetch=1, grid=(), in_specs=in_vmem(2), out_specs=pl.BlockSpec(memory_space=pltpu.VMEM)
        ),
        out_shape=jax.ShapeDtypeStruct((2, 4 * size, 4 * size), F32),
        compiler_params=params(),
        cost_estimate=pl.CostEstimate(flops=0, bytes_accessed=4 * MIB, transcendentals=0),
        name="square",
    )(core, mine, oth)


def order_kernel(chip, *refs):
    h = refs[0].shape[0]
    for bits, ref in enumerate(refs[:-1]):
        refs[-1][pl.ds(pl.multiple_of((chip[0] ^ bits) * h, 8), h)] = ref[...]


def order(chip, came):
    h, width = came[0].shape
    return pl.pallas_call(
        order_kernel,
        grid_spec=pltpu.PrefetchScalarGridSpec(
            num_scalar_prefetch=1, grid=(), in_specs=in_vmem(len(came)), out_specs=pl.BlockSpec(memory_space=pltpu.VMEM)
        ),
        out_shape=jax.ShapeDtypeStruct((len(came) * h, width), F32),
        compiler_params=params(),
        cost_estimate=pl.CostEstimate(flops=0, bytes_accessed=2 * MIB, transcendentals=0),
        name="order",
    )(chip, *came)


def place_kernel(wanted, core, y0, y1, z0, z1, oth, out):
    rows, half = ITEMS // 2, y0.shape[2]
    part = out.shape[1]
    for step in range(2 * rows // part):

        @pl.when(pl.program_id(0) == step)
        def _():
            j = step * part // rows
            for q in range(step * part % rows, step * part % rows + part):
                keep = wanted[j * rows + q] != 0
                which, at = where_is(j, 0, q, rows)
                mine = jnp.where(keep, -((y0, y1)[which][at] + (z0, z1)[which][at]), 0.0)
                other = jnp.where(keep, -oth[j * rows + q], 0.0)
                out[0, q % part, :, :half] = jnp.where(core[0] == 0, mine, other)
                out[0, q % part, :, half:] = jnp.where(core[0] == 0, other, mine)


def place(wanted, core, ys, recv, oth):
    _, size, half = ys[0].shape
    rows = ITEMS // 2
    return pl.pallas_call(
        place_kernel,
        grid_spec=pltpu.PrefetchScalarGridSpec(
            num_scalar_prefetch=2,
            grid=(4,),
            in_specs=in_vmem(5),
            out_specs=pl.BlockSpec((1, rows // 2, size, 2 * half), lambda i, *_: (i // 2, i % 2, 0, 0)),
        ),
        out_shape=jax.ShapeDtypeStruct((2, rows, size, 2 * half), F32),
        compiler_params=params(),
        cost_estimate=pl.CostEstimate(flops=0, bytes_accessed=5 * MIB, transcendentals=0),
        name="place",
    )(wanted, core, *ys, *recv, oth)


def any_mesh(sigma_anc, panel, pattern, linv):
    high = lax.Precision.HIGH
    einsum = functools.partial(jnp.einsum, precision=high, preferred_element_type=F32)
    rows, cols = lax.axis_size("row"), lax.axis_size("col")
    row_ids = jnp.arange(sigma_anc.shape[0], dtype=jnp.int32) * rows + lax.axis_index("row")
    col_ids = jnp.arange(sigma_anc.shape[1], dtype=jnp.int32) * cols + lax.axis_index("col")
    wanted = jnp.any(pattern[:, :, None] == row_ids, axis=1).astype(F32)[:, :, None, None]
    u = einsum("sqiw,swv->sqiv", panel, linv) * wanted
    pick = (col_ids[:, None] == row_ids[None, :]).astype(F32)
    u_cols = lax.psum(jnp.einsum("kq,sqiw->skiw", pick, u, precision=lax.Precision.HIGHEST), "row")
    y = lax.psum(einsum("qkij,skjw->sqiw", sigma_anc, u_cols), "col") * wanted
    total = lax.psum(einsum("sqiw,sqiv->swv", u, y), "row")
    return -y, einsum("siw,siv->swv", linv, linv) + total


def ring_place(chip, chips):
    z, x = chip // 2, chip % 2
    return jnp.where(x == 0, z, chips - 1 - z)


def ring_chip(place, chips):
    place = place % chips
    return jnp.where(place < chips // 2, 2 * place, 2 * (chips - 1 - place) + 1)


def pair_rows(sigma_anc, panel, linv, wanted):
    supers, rows, size, width = panel.shape
    half = width // 2
    n_row = lax.axis_size("row")
    chips = n_row // 2
    me, plane = lax.axis_index("row"), lax.axis_index("col")
    chip, core = me // 2, me % 2
    place_here = ring_place(chip, chips)
    across = [(i, i ^ 1) for i in range(n_row)]
    pair = [(0, 1), (1, 0)]
    order = [2 * q for q in range(chips // 2)] + [2 * (chips - 1 - q) + 1 for q in range(chips // 2, chips)]
    around = []
    for q in range(chips):
        around.append((2 * order[q], 2 * order[(q + 1) % chips]))
        around.append((2 * order[q] + 1, 2 * order[(q - 1) % chips] + 1))

    near, away = update(core[None], far(panel), far(linv))
    away_oth = lax.ppermute(away, "row", across)
    first = jnp.where(core == plane, near, away_oth)
    wanted_here = jnp.where(plane == 0, wanted[0], wanted[1]).reshape(-1)
    wanted_rows = jnp.where(core == 0, wanted, wanted[::-1])
    wanted_rows = lax.dynamic_index_in_dim(wanted_rows, chip, 1, keepdims=False).reshape(-1)
    held = [first[:rows], first[rows:]]
    accs = [jnp.zeros((count, size, half), F32) for count in (FIRST, 2 * ITEMS - FIRST)]
    span = width // (2 * chips)
    share = lax.dynamic_slice_in_dim(linv, (chip * 2 + plane) * span, span, axis=1)
    waiting = []
    s_own = far(sigma_anc)
    s_oth = near_oth = None
    for step in range(chips):
        origin = ring_chip(place_here + jnp.where(core == 0, -step, step), chips)
        blocks = tuple(held)
        if step < chips - 1:
            came = held[0]
            held[0] = lax.ppermute(came, "row", around)
            while len(waiting) > 1:
                accs = add_columns(*waiting.pop(0), accs)
            if step == 3:
                us = [far(u) for u in us]
                wanted_rows, share, held[1], *us = lax.optimization_barrier((wanted_rows, share, held[1], *us))
            sent, _, *accs = lax.optimization_barrier((held[1], came, *accs))
            held[1] = lax.ppermute(sent, "row", around)
        if s_oth is None:
            s_sent, near_sent, _ = lax.optimization_barrier((sigma_anc, near, away_oth))
            s_oth = lax.ppermute(s_sent, "row", across)
            near_oth = lax.ppermute(near_sent, "row", across)
            us = [near, away, away_oth, near_oth]
        waiting.append((wanted_here, origin[None], *blocks, s_own, s_oth))
    for last in waiting:
        accs = add_columns(*last, accs)

    parts = inner(wanted_rows, jnp.stack([core, chip]), [us[k] for k in (0, 2, 1, 3)], share, accs, chips)
    total, recv, y_oth = all_sum(parts, accs, chip, chips, pair, across)
    total = total.reshape(-1, size, size)
    total_oth = lax.ppermute(total, "row", across)
    sigma_sj = place(wanted_rows[:ITEMS], core[None], accs, recv, y_oth)
    return sigma_sj, square(core[None], total, total_oth)


def all_sum(parts, ys, chip, chips, pair, across):
    def flip(bits):
        return [(i, i ^ (2 * bits)) for i in range(2 * chips)]

    most = lax.ppermute(ys[0], "col", pair)
    mine = parts[0]
    for bits in range(1, chips):
        mine = mine + lax.ppermute(parts[bits], "row", flip(bits))
    mine, most = lax.optimization_barrier((mine, most))
    mine = mine + lax.ppermute(mine, "col", pair)
    y_oth = lax.ppermute(ys[0][:ITEMS] + most[:ITEMS], "row", across)
    mine, sent, y_oth = lax.optimization_barrier((mine, ys[1], y_oth))
    rest = lax.ppermute(sent, "col", pair)
    came = [mine] + [lax.ppermute(mine, "row", flip(bits)) for bits in range(1, chips)]
    *came, rest = lax.optimization_barrier((*came, rest))
    return order(chip[None], came), (most, rest), y_oth


def local(sigma_anc, panel, pattern, linv):
    n_row, n_col = lax.axis_size("row"), lax.axis_size("col")
    rows = sigma_anc.shape[0]
    supers = panel.shape[0]
    if (n_row, n_col, rows * supers) != (16, 2, ITEMS):
        return any_mesh(sigma_anc, panel, pattern, linv)
    chips = n_row // 2
    e = jnp.arange(ITEMS, dtype=jnp.int32)
    ids = (
        (e % rows)[None, None, :] * n_row
        + 2 * jnp.arange(chips, dtype=jnp.int32)[None, :, None]
        + jnp.arange(2, dtype=jnp.int32)[:, None, None]
    )
    hit = jnp.any(pattern[:, None, None, None, :] == ids[None, ..., None], axis=-1)
    wanted = jnp.where(e // rows == 0, hit[0], hit[1])
    return pair_rows(sigma_anc, panel, linv, wanted.astype(jnp.int32))


def solution(mesh):
    return jax.shard_map(
        local,
        mesh=mesh,
        in_specs=(P("row", "col", None, None), P(None, "row", None, None), P(), P()),
        out_specs=(P(None, "row", None, None), P()),
        check_vma=False,
    )
```

```python
import functools

import jax
import jax.numpy as jnp
from jax import lax
from jax.experimental import pallas as pl
from jax.experimental.pallas import tpu as pltpu
from jax.sharding import PartitionSpec as P

F32 = jnp.float32
BF16 = jnp.bfloat16
MIB = 1 << 20


def split(x):
    hi = x.astype(BF16)
    return hi, (x - hi.astype(F32)).astype(BF16)


def dot3(a, b, a_axis=1, b_axis=0):
    left = jnp.concatenate([a[0], a[1], a[0]], axis=a_axis)
    right = jnp.concatenate([b[0], b[0], b[1]], axis=b_axis)
    dims = (((a_axis,), (b_axis,)), ((), ()))
    return lax.dot_general(left, right, dims, preferred_element_type=F32)


def three(a, b):
    dot = functools.partial(jnp.dot, preferred_element_type=F32)
    return dot(a[0], b[0]) + (dot(a[0], b[1]) + dot(a[1], b[0]))


ITEMS = 8
FIRST = 9


def where_is(j, source, q, rows):
    n = (1 - source) * 2 * rows + j * rows + q
    return (0, n) if n < FIRST else (1, n - FIRST)


def in_vmem(count):
    return [pl.BlockSpec(memory_space=pltpu.VMEM)] * count


def far(x):
    return pltpu.with_memory_space_constraint(x, pltpu.HBM)


def params(mib=24):
    return pltpu.CompilerParams(vmem_limit_bytes=mib * MIB)


def update_kernel(core, panel, linv, near, away, rows_in, low_in, arrived):
    supers, rows, size, width = panel.shape
    half = width // 2
    swapped = core[0] == 1

    def copies(j):
        yield pltpu.make_async_copy(linv.at[j], low_in.at[j], arrived.at[j, rows])
        for q in range(rows):
            yield pltpu.make_async_copy(panel.at[j, q], rows_in.at[j, q], arrived.at[j, q])

    for j in range(supers):
        for copy in copies(j):
            copy.start()
    for j in range(supers):
        for copy in copies(j):
            copy.wait()
        left = split(rows_in[j].reshape(rows * size, width))
        first = three(left, split(low_in[j, :, :half]))
        second = three([x[:, half:] for x in left], split(low_in[j, half:, half:]))
        here, there = jnp.where(swapped, second, first), jnp.where(swapped, first, second)
        near[j * rows:(j + 1) * rows] = here.reshape(rows, size, half)
        away[j * rows:(j + 1) * rows] = there.reshape(rows, size, half)


def update(core, panel, linv):
    supers, rows, size, width = panel.shape
    hbm = pl.BlockSpec(memory_space=pltpu.HBM)
    return pl.pallas_call(
        update_kernel,
        grid_spec=pltpu.PrefetchScalarGridSpec(
            num_scalar_prefetch=1,
            grid=(),
            in_specs=[hbm, hbm],
            out_specs=in_vmem(2),
            scratch_shapes=[
                pltpu.VMEM(panel.shape, F32),
                pltpu.VMEM(linv.shape, F32),
                pltpu.SemaphoreType.DMA((supers, rows + 1)),
            ],
        ),
        out_shape=[jax.ShapeDtypeStruct((ITEMS, size, width // 2), F32)] * 2,
        compiler_params=params(32),
        cost_estimate=pl.CostEstimate(
            flops=6 * supers * rows * size * width * width, bytes_accessed=6 * MIB, transcendentals=0
        ),
        name="update",
    )(core, panel, linv)


def column_kernel(given, ahead, wanted, chip, u0, u1, own, oth, *refs):
    accs, refs = refs[:2], refs[2:]
    if given:
        blocks, refs = refs[0], refs[1:]
    outs, refs = refs[:2], refs[2:]
    if ahead:
        later, refs = refs[0], refs[1:]
    if not given:
        blocks, refs = refs[0], refs[1:]
    arrived = refs[0]
    rows, cols, size, _ = own.shape
    items, _, width = u0.shape

    def wants(i, turn=0):
        at = chip[turn] * ITEMS + i
        return wanted[at] != 0, wanted[at + items] != 0

    def each(i, turn, task):
        first, second = wants(i, turn)
        column = i * (cols // items) + chip[turn]

        @pl.when(first | second)
        def _():
            for source, ref in enumerate((own, oth)):
                target = (later if turn else blocks).at[i, source]
                task(pltpu.make_async_copy(ref.at[:, column], target, arrived.at[turn, i, source]))

    def start(copy):
        copy.start()

    def wait(copy):
        copy.wait()

    for turn in ([] if given else [0]) + ([1] if ahead else []):
        for i in range(items):
            each(i, turn, start)

    for acc, out in zip(accs, outs):
        out[...] = acc[...]

    def body(i, carry):
        first, second = wants(i)
        if not given:
            each(i, 0, wait)

        @pl.when(first | second)
        def _():
            pair = [jnp.where(first, u0[i], 0.0), jnp.where(second, u1[i], 0.0)]
            right = split(jnp.concatenate(pair, axis=1))
            left = split(blocks[i].reshape(2 * rows * size, size))
            product = dot3(left, right).reshape(2, rows, size, 2 * width)
            for j in range(2):
                for source in range(2):
                    for q in range(rows):
                        which, at = where_is(j, source, q, rows)
                        outs[which][at] += product[source, q, :, j * width:(j + 1) * width]

        return carry

    lax.fori_loop(0, items, body, 0)
    if ahead:
        for i in range(items):
            each(i, 1, wait)


def add_columns(wanted, chip, u0, u1, own, oth, accs, blocks=None, chip_later=None):
    items, size, width = u0.shape
    rows = own.shape[0]
    hbm = pl.BlockSpec(memory_space=pltpu.HBM)
    given, ahead = blocks is not None, chip_later is not None
    shape = (items, 2, rows, size, size)
    chips = jnp.concatenate([chip, chip_later]) if ahead else chip
    result = pl.pallas_call(
        functools.partial(column_kernel, given, ahead),
        grid_spec=pltpu.PrefetchScalarGridSpec(
            num_scalar_prefetch=2,
            grid=(),
            in_specs=in_vmem(2) + [hbm, hbm] + in_vmem(2 + given),
            out_specs=in_vmem(2 + ahead),
            scratch_shapes=([] if given else [pltpu.VMEM(shape, F32)]) + [
                pltpu.SemaphoreType.DMA((2, items, 2)),
            ],
        ),
        out_shape=[jax.ShapeDtypeStruct(x, F32) for x in [acc.shape for acc in accs] + [shape] * ahead],
        input_output_aliases={6 + i: i for i in range(2)},
        compiler_params=params(28),
        cost_estimate=pl.CostEstimate(
            flops=24 * items * rows * size * size * width, bytes_accessed=6 * MIB, transcendentals=0
        ),
        name="add_columns",
    )(wanted, chips, u0, u1, own, oth, *accs, *([blocks] if given else []))
    return (result[:2], result[2]) if ahead else result


def inner_kernel(wanted, here_is, *refs):
    us, (share, y0, y1), outs, (held, tiles, arrived) = refs[:4], refs[4:7], refs[7:15], refs[15:]
    _, size, half = y0.shape
    rows = ITEMS // 2
    core = here_is

    def each(k, j, task):
        for q in range(rows):
            e = j * rows + q
            for source in range(2):

                @pl.when(wanted[source * ITEMS + e] != 0)
                def _():
                    task(pltpu.make_async_copy(us[k + source].at[e], held.at[k + source, e], arrived.at[k + source, e]))

    for j in range(2):
        for k in (0, 2):
            each(k, j, lambda copy: copy.start())

    def stack(j, k, start, begin, end):
        parts = [
            jnp.where(wanted[s * ITEMS + j * rows + q] != 0, held[k + s, j * rows + q, :, begin:end], 0.0)
            for s in range(2)
            for q in range(rows)
        ]
        return split(jnp.concatenate(parts + [start[:, begin:end]], axis=0))

    def put(k, tile):
        tiles[k * size:(k + 1) * size] = tile

    for j in range(2):
        low, high = share[j, :, :half], share[j, :, half:]
        here, there = jnp.where(core[0] == 1, high, low), jnp.where(core[0] == 1, low, high)
        right = []
        for source in range(2):
            for q in range(rows):
                which, at = where_is(j, source, q, rows)
                y = (y0, y1)[which][at]
                right.append(jnp.where(wanted[source * ITEMS + j * rows + q] != 0, y, 0.0))
        right = split(jnp.concatenate(right + [here], axis=0))
        first = 5 * j
        each(0, j, lambda copy: copy.wait())
        diag = dot3(stack(j, 0, here, 0, half), right, 0, 0)
        put(first, diag[:size, :size])
        put(first + 1, diag[size:, :size])
        put(first + 2, diag[size:, size:])
        each(2, j, lambda copy: copy.wait())

        @pl.when(core[0] == 0)
        def _():
            cross = dot3(stack(j, 2, there, 0, size), right, 0, 0)
            put(first + 3, cross[:, :size])
            put(first + 4, cross[:, size:])

        @pl.when(core[0] != 0)
        def _():
            cross = dot3(stack(j, 2, there, 0, half), [x[:, size:] for x in right], 0, 0)
            put(first + 3, cross[:size])
            put(first + 4, cross[size:])

    h = outs[0].shape[0]
    for bits, out in enumerate(outs):
        out[...] = tiles[pl.ds(pl.multiple_of((here_is[1] ^ bits) * h, 8), h)]


def inner(wanted, here_is, us, share, ys, chips):
    _, size, half = ys[0].shape
    hbm = pl.BlockSpec(memory_space=pltpu.HBM)
    return pl.pallas_call(
        inner_kernel,
        grid_spec=pltpu.PrefetchScalarGridSpec(
            num_scalar_prefetch=2,
            grid=(),
            in_specs=[hbm] * 4 + in_vmem(3),
            out_specs=in_vmem(chips),
            scratch_shapes=[
                pltpu.VMEM((4, *us[0].shape), F32),
                pltpu.VMEM((10 * size, size), F32),
                pltpu.SemaphoreType.DMA((4, ITEMS)),
            ],
        ),
        out_shape=[jax.ShapeDtypeStruct((10 * size // chips, size), F32)] * chips,
        compiler_params=params(36),
        cost_estimate=pl.CostEstimate(
            flops=18 * ITEMS * size * half * half, bytes_accessed=8 * MIB, transcendentals=0
        ),
        name="inner",
    )(wanted, here_is, *us, share, *ys)


def square_kernel(core, mine, oth, out):
    size = mine.shape[1]

    def put(j, row, col, tile):
        out[j, row * size:(row + 1) * size, col * size:(col + 1) * size] = tile

    for j in range(2):
        for c in range(2):
            diag0, below, diag1, one, two = (jnp.where(core[0] == c, mine[5 * j + k], oth[5 * j + k]) for k in range(5))
            put(j, 2 * c, 2 * c, diag0)
            put(j, 2 * c + 1, 2 * c, below)
            put(j, 2 * c, 2 * c + 1, below.T)
            put(j, 2 * c + 1, 2 * c + 1, diag1)
            for t, tile in enumerate((one, two)):
                row, col = (2, t) if c == 0 else (t, 3)
                put(j, row, col, tile)
                put(j, col, row, tile.T)


def square(core, mine, oth):
    size = mine.shape[1]
    return pl.pallas_call(
        square_kernel,
        grid_spec=pltpu.PrefetchScalarGridSpec(
            num_scalar_prefetch=1, grid=(), in_specs=in_vmem(2), out_specs=pl.BlockSpec(memory_space=pltpu.VMEM)
        ),
        out_shape=jax.ShapeDtypeStruct((2, 4 * size, 4 * size), F32),
        compiler_params=params(),
        cost_estimate=pl.CostEstimate(flops=0, bytes_accessed=4 * MIB, transcendentals=0),
        name="square",
    )(core, mine, oth)


def order_kernel(chip, *refs):
    h = refs[0].shape[0]
    for bits, ref in enumerate(refs[:-1]):
        refs[-1][pl.ds(pl.multiple_of((chip[0] ^ bits) * h, 8), h)] = ref[...]


def order(chip, came):
    h, width = came[0].shape
    return pl.pallas_call(
        order_kernel,
        grid_spec=pltpu.PrefetchScalarGridSpec(
            num_scalar_prefetch=1, grid=(), in_specs=in_vmem(len(came)), out_specs=pl.BlockSpec(memory_space=pltpu.VMEM)
        ),
        out_shape=jax.ShapeDtypeStruct((len(came) * h, width), F32),
        compiler_params=params(),
        cost_estimate=pl.CostEstimate(flops=0, bytes_accessed=2 * MIB, transcendentals=0),
        name="order",
    )(chip, *came)


def place_kernel(wanted, core, y0, y1, z0, z1, oth, out):
    rows, half = ITEMS // 2, y0.shape[2]
    part = out.shape[1]
    for step in range(2 * rows // part):

        @pl.when(pl.program_id(0) == step)
        def _():
            j = step * part // rows
            for q in range(step * part % rows, step * part % rows + part):
                keep = wanted[j * rows + q] != 0
                which, at = where_is(j, 0, q, rows)
                mine = jnp.where(keep, -((y0, y1)[which][at] + (z0, z1)[which][at]), 0.0)
                other = jnp.where(keep, -oth[j * rows + q], 0.0)
                out[0, q % part, :, :half] = jnp.where(core[0] == 0, mine, other)
                out[0, q % part, :, half:] = jnp.where(core[0] == 0, other, mine)


def place(wanted, core, ys, recv, oth):
    _, size, half = ys[0].shape
    rows = ITEMS // 2
    return pl.pallas_call(
        place_kernel,
        grid_spec=pltpu.PrefetchScalarGridSpec(
            num_scalar_prefetch=2,
            grid=(4,),
            in_specs=in_vmem(5),
            out_specs=pl.BlockSpec((1, rows // 2, size, 2 * half), lambda i, *_: (i // 2, i % 2, 0, 0)),
        ),
        out_shape=jax.ShapeDtypeStruct((2, rows, size, 2 * half), F32),
        compiler_params=params(),
        cost_estimate=pl.CostEstimate(flops=0, bytes_accessed=5 * MIB, transcendentals=0),
        name="place",
    )(wanted, core, *ys, *recv, oth)


def any_mesh(sigma_anc, panel, pattern, linv):
    high = lax.Precision.HIGH
    einsum = functools.partial(jnp.einsum, precision=high, preferred_element_type=F32)
    rows, cols = lax.axis_size("row"), lax.axis_size("col")
    row_ids = jnp.arange(sigma_anc.shape[0], dtype=jnp.int32) * rows + lax.axis_index("row")
    col_ids = jnp.arange(sigma_anc.shape[1], dtype=jnp.int32) * cols + lax.axis_index("col")
    wanted = jnp.any(pattern[:, :, None] == row_ids, axis=1).astype(F32)[:, :, None, None]
    u = einsum("sqiw,swv->sqiv", panel, linv) * wanted
    pick = (col_ids[:, None] == row_ids[None, :]).astype(F32)
    u_cols = lax.psum(jnp.einsum("kq,sqiw->skiw", pick, u, precision=lax.Precision.HIGHEST), "row")
    y = lax.psum(einsum("qkij,skjw->sqiw", sigma_anc, u_cols), "col") * wanted
    total = lax.psum(einsum("sqiw,sqiv->swv", u, y), "row")
    return -y, einsum("siw,siv->swv", linv, linv) + total


def ring_place(chip, chips):
    z, x = chip // 2, chip % 2
    return jnp.where(x == 0, z, chips - 1 - z)


def ring_chip(place, chips):
    place = place % chips
    return jnp.where(place < chips // 2, 2 * place, 2 * (chips - 1 - place) + 1)


def pair_rows(sigma_anc, panel, linv, wanted):
    supers, rows, size, width = panel.shape
    half = width // 2
    n_row = lax.axis_size("row")
    chips = n_row // 2
    me, plane = lax.axis_index("row"), lax.axis_index("col")
    chip, core = me // 2, me % 2
    place_here = ring_place(chip, chips)
    across = [(i, i ^ 1) for i in range(n_row)]
    pair = [(0, 1), (1, 0)]
    order = [2 * q for q in range(chips // 2)] + [2 * (chips - 1 - q) + 1 for q in range(chips // 2, chips)]
    around = []
    for q in range(chips):
        around.append((2 * order[q], 2 * order[(q + 1) % chips]))
        around.append((2 * order[q] + 1, 2 * order[(q - 1) % chips] + 1))

    near, away = update(core[None], far(panel), far(linv))
    away_oth = lax.ppermute(away, "row", across)
    first = jnp.where(core == plane, near, away_oth)
    wanted_here = jnp.where(plane == 0, wanted[0], wanted[1]).reshape(-1)
    wanted_rows = jnp.where(core == 0, wanted, wanted[::-1])
    wanted_rows = lax.dynamic_index_in_dim(wanted_rows, chip, 1, keepdims=False).reshape(-1)
    held = [first[:rows], first[rows:]]
    accs = [jnp.zeros((count, size, half), F32) for count in (FIRST, 2 * ITEMS - FIRST)]
    span = width // (2 * chips)
    share = lax.dynamic_slice_in_dim(linv, (chip * 2 + plane) * span, span, axis=1)
    waiting = []
    s_own = far(sigma_anc)
    s_oth = near_oth = None
    for step in range(chips):
        origin = ring_chip(place_here + jnp.where(core == 0, -step, step), chips)
        blocks = tuple(held)
        if step < chips - 1:
            came = held[0]
            held[0] = lax.ppermute(came, "row", around)
            while len(waiting) > 1:
                accs = add_columns(*waiting.pop(0), accs)
            if step == 3:
                us = [far(u) for u in us]
                wanted_rows, share, held[1], *us = lax.optimization_barrier((wanted_rows, share, held[1], *us))
            sent, _, *accs = lax.optimization_barrier((held[1], came, *accs))
            held[1] = lax.ppermute(sent, "row", around)
        if s_oth is None:
            s_sent, near_sent, _ = lax.optimization_barrier((sigma_anc, near, away_oth))
            s_oth = lax.ppermute(s_sent, "row", across)
            near_oth = lax.ppermute(near_sent, "row", across)
            us = [near, away, away_oth, near_oth]
        waiting.append((wanted_here, origin[None], *blocks, s_own, s_oth))
    for early in waiting[:-2]:
        accs = add_columns(*early, accs)
    accs, kept = add_columns(*waiting[-2], accs, chip_later=waiting[-1][1])
    accs = add_columns(*waiting[-1], accs, blocks=kept)

    parts = inner(wanted_rows, jnp.stack([core, chip]), [us[k] for k in (0, 2, 1, 3)], share, accs, chips)
    total, recv, y_oth = all_sum(parts, accs, chip, chips, pair, across)
    total = total.reshape(-1, size, size)
    total_oth = lax.ppermute(total, "row", across)
    sigma_sj = place(wanted_rows[:ITEMS], core[None], accs, recv, y_oth)
    return sigma_sj, square(core[None], total, total_oth)


def all_sum(parts, ys, chip, chips, pair, across):
    def flip(bits):
        return [(i, i ^ (2 * bits)) for i in range(2 * chips)]

    most = lax.ppermute(ys[0], "col", pair)
    mine = parts[0]
    for bits in range(1, chips):
        mine = mine + lax.ppermute(parts[bits], "row", flip(bits))
    mine, most = lax.optimization_barrier((mine, most))
    mine = mine + lax.ppermute(mine, "col", pair)
    y_oth = lax.ppermute(ys[0][:ITEMS] + most[:ITEMS], "row", across)
    mine, sent, y_oth = lax.optimization_barrier((mine, ys[1], y_oth))
    rest = lax.ppermute(sent, "col", pair)
    came = [mine] + [lax.ppermute(mine, "row", flip(bits)) for bits in range(1, chips)]
    *came, rest = lax.optimization_barrier((*came, rest))
    return order(chip[None], came), (most, rest), y_oth


def local(sigma_anc, panel, pattern, linv):
    n_row, n_col = lax.axis_size("row"), lax.axis_size("col")
    rows = sigma_anc.shape[0]
    supers = panel.shape[0]
    if (n_row, n_col, rows * supers) != (16, 2, ITEMS):
        return any_mesh(sigma_anc, panel, pattern, linv)
    chips = n_row // 2
    e = jnp.arange(ITEMS, dtype=jnp.int32)
    ids = (
        (e % rows)[None, None, :] * n_row
        + 2 * jnp.arange(chips, dtype=jnp.int32)[None, :, None]
        + jnp.arange(2, dtype=jnp.int32)[:, None, None]
    )
    hit = jnp.any(pattern[:, None, None, None, :] == ids[None, ..., None], axis=-1)
    wanted = jnp.where(e // rows == 0, hit[0], hit[1])
    return pair_rows(sigma_anc, panel, linv, wanted.astype(jnp.int32))


def solution(mesh):
    return jax.shard_map(
        local,
        mesh=mesh,
        in_specs=(P("row", "col", None, None), P(None, "row", None, None), P(), P()),
        out_specs=(P(None, "row", None, None), P()),
        check_vma=False,
    )
```

```python
import functools

import jax
import jax.numpy as jnp
from jax import lax
from jax.experimental import pallas as pl
from jax.experimental.pallas import tpu as pltpu
from jax.sharding import PartitionSpec as P

F32 = jnp.float32
BF16 = jnp.bfloat16
MIB = 1 << 20


def split(x):
    hi = x.astype(BF16)
    return hi, (x - hi.astype(F32)).astype(BF16)


def dot3(a, b, a_axis=1, b_axis=0):
    left = jnp.concatenate([a[0], a[1], a[0]], axis=a_axis)
    right = jnp.concatenate([b[0], b[0], b[1]], axis=b_axis)
    dims = (((a_axis,), (b_axis,)), ((), ()))
    return lax.dot_general(left, right, dims, preferred_element_type=F32)


def three(a, b):
    dot = functools.partial(jnp.dot, preferred_element_type=F32)
    return dot(a[0], b[0]) + (dot(a[0], b[1]) + dot(a[1], b[0]))


ITEMS = 8
FIRST = 9


def where_is(j, source, q, rows):
    n = (1 - source) * 2 * rows + j * rows + q
    return (0, n) if n < FIRST else (1, n - FIRST)


def in_vmem(count):
    return [pl.BlockSpec(memory_space=pltpu.VMEM)] * count


def far(x):
    return pltpu.with_memory_space_constraint(x, pltpu.HBM)


def params(mib=24):
    return pltpu.CompilerParams(vmem_limit_bytes=mib * MIB)


def update_kernel(core, panel, linv, near, away, rows_in, low_in, arrived):
    supers, rows, size, width = panel.shape
    half = width // 2
    swapped = core[0] == 1

    def copies(j):
        yield pltpu.make_async_copy(linv.at[j], low_in.at[j], arrived.at[j, rows])
        for q in range(rows):
            yield pltpu.make_async_copy(panel.at[j, q], rows_in.at[j, q], arrived.at[j, q])

    for j in range(supers):
        for copy in copies(j):
            copy.start()
    for j in range(supers):
        for copy in copies(j):
            copy.wait()
        left = split(rows_in[j].reshape(rows * size, width))
        first = three(left, split(low_in[j, :, :half]))
        second = three([x[:, half:] for x in left], split(low_in[j, half:, half:]))
        here, there = jnp.where(swapped, second, first), jnp.where(swapped, first, second)
        near[j * rows:(j + 1) * rows] = here.reshape(rows, size, half)
        away[j * rows:(j + 1) * rows] = there.reshape(rows, size, half)


def update(core, panel, linv):
    supers, rows, size, width = panel.shape
    hbm = pl.BlockSpec(memory_space=pltpu.HBM)
    return pl.pallas_call(
        update_kernel,
        grid_spec=pltpu.PrefetchScalarGridSpec(
            num_scalar_prefetch=1,
            grid=(),
            in_specs=[hbm, hbm],
            out_specs=in_vmem(2),
            scratch_shapes=[
                pltpu.VMEM(panel.shape, F32),
                pltpu.VMEM(linv.shape, F32),
                pltpu.SemaphoreType.DMA((supers, rows + 1)),
            ],
        ),
        out_shape=[jax.ShapeDtypeStruct((ITEMS, size, width // 2), F32)] * 2,
        compiler_params=params(32),
        cost_estimate=pl.CostEstimate(
            flops=6 * supers * rows * size * width * width, bytes_accessed=6 * MIB, transcendentals=0
        ),
        name="update",
    )(core, panel, linv)


def column_kernel(given, ahead, wanted, chip, u0, u1, own, oth, *refs):
    accs, refs = refs[:2], refs[2:]
    if given:
        blocks, refs = refs[0], refs[1:]
    outs, refs = refs[:2], refs[2:]
    if ahead:
        later, refs = refs[0], refs[1:]
    if not given:
        blocks, refs = refs[0], refs[1:]
    arrived = refs[0]
    rows, cols, size, _ = own.shape
    items, _, width = u0.shape

    def wants(i, turn=0):
        at = chip[turn] * ITEMS + i
        return wanted[at] != 0, wanted[at + items] != 0

    def each(i, turn, task):
        first, second = wants(i, turn)
        column = i * (cols // items) + chip[turn]

        @pl.when(first | second)
        def _():
            for source, ref in enumerate((own, oth)):
                target = (later if turn else blocks).at[i, source]
                task(pltpu.make_async_copy(ref.at[:, column], target, arrived.at[turn, i, source]))

    def start(copy):
        copy.start()

    def wait(copy):
        copy.wait()

    for turn in ([] if given else [0]) + ([1] if ahead else []):
        for i in range(items):
            each(i, turn, start)

    for acc, out in zip(accs, outs):
        out[...] = acc[...]

    def body(i, carry):
        first, second = wants(i)
        if not given:
            each(i, 0, wait)

        @pl.when(first | second)
        def _():
            pair = [jnp.where(first, u0[i], 0.0), jnp.where(second, u1[i], 0.0)]
            right = split(jnp.concatenate(pair, axis=1))
            left = split(blocks[i].reshape(2 * rows * size, size))
            product = dot3(left, right).reshape(2, rows, size, 2 * width)
            for j in range(2):
                for source in range(2):
                    for q in range(rows):
                        which, at = where_is(j, source, q, rows)
                        outs[which][at] += product[source, q, :, j * width:(j + 1) * width]

        return carry

    lax.fori_loop(0, items, body, 0)
    if ahead:
        for i in range(items):
            each(i, 1, wait)


def add_columns(wanted, chip, u0, u1, own, oth, accs, blocks=None, chip_later=None):
    items, size, width = u0.shape
    rows = own.shape[0]
    hbm = pl.BlockSpec(memory_space=pltpu.HBM)
    given, ahead = blocks is not None, chip_later is not None
    shape = (items, 2, rows, size, size)
    chips = jnp.concatenate([chip, chip_later]) if ahead else chip
    result = pl.pallas_call(
        functools.partial(column_kernel, given, ahead),
        grid_spec=pltpu.PrefetchScalarGridSpec(
            num_scalar_prefetch=2,
            grid=(),
            in_specs=in_vmem(2) + [hbm, hbm] + in_vmem(2 + given),
            out_specs=in_vmem(2 + ahead),
            scratch_shapes=([] if given else [pltpu.VMEM(shape, F32)]) + [
                pltpu.SemaphoreType.DMA((2, items, 2)),
            ],
        ),
        out_shape=[jax.ShapeDtypeStruct(x, F32) for x in [acc.shape for acc in accs] + [shape] * ahead],
        input_output_aliases={6 + i: i for i in range(2)},
        compiler_params=params(28),
        cost_estimate=pl.CostEstimate(
            flops=24 * items * rows * size * size * width, bytes_accessed=6 * MIB, transcendentals=0
        ),
        name="add_columns",
    )(wanted, chips, u0, u1, own, oth, *accs, *([blocks] if given else []))
    return (result[:2], result[2]) if ahead else result


def inner_kernel(wanted, here_is, *refs):
    us, (share, y0, y1), outs, (held, tiles, arrived) = refs[:4], refs[4:7], refs[7:15], refs[15:]
    _, size, half = y0.shape
    rows = ITEMS // 2
    core = here_is

    def each(k, j, task):
        for q in range(rows):
            e = j * rows + q
            for source in range(2):

                @pl.when(wanted[source * ITEMS + e] != 0)
                def _():
                    task(pltpu.make_async_copy(us[k + source].at[e], held.at[k + source, e], arrived.at[k + source, e]))

    for j in range(2):
        for k in (0, 2):
            each(k, j, lambda copy: copy.start())

    def stack(j, k, start, begin, end):
        parts = [
            jnp.where(wanted[s * ITEMS + j * rows + q] != 0, held[k + s, j * rows + q, :, begin:end], 0.0)
            for s in range(2)
            for q in range(rows)
        ]
        return split(jnp.concatenate(parts + [start[:, begin:end]], axis=0))

    def put(k, tile):
        tiles[k * size:(k + 1) * size] = tile

    for j in range(2):
        low, high = share[j, :, :half], share[j, :, half:]
        here, there = jnp.where(core[0] == 1, high, low), jnp.where(core[0] == 1, low, high)
        right = []
        for source in range(2):
            for q in range(rows):
                which, at = where_is(j, source, q, rows)
                y = (y0, y1)[which][at]
                right.append(jnp.where(wanted[source * ITEMS + j * rows + q] != 0, y, 0.0))
        right = split(jnp.concatenate(right + [here], axis=0))
        first = 5 * j
        each(0, j, lambda copy: copy.wait())
        diag = dot3(stack(j, 0, here, 0, half), right, 0, 0)
        put(first, diag[:size, :size])
        put(first + 1, diag[size:, :size])
        put(first + 2, diag[size:, size:])
        each(2, j, lambda copy: copy.wait())

        @pl.when(core[0] == 0)
        def _():
            cross = dot3(stack(j, 2, there, 0, size), right, 0, 0)
            put(first + 3, cross[:, :size])
            put(first + 4, cross[:, size:])

        @pl.when(core[0] != 0)
        def _():
            cross = dot3(stack(j, 2, there, 0, half), [x[:, size:] for x in right], 0, 0)
            put(first + 3, cross[:size])
            put(first + 4, cross[size:])

    h = outs[0].shape[0]
    for bits, out in enumerate(outs):
        out[...] = tiles[pl.ds(pl.multiple_of((here_is[1] ^ bits) * h, 8), h)]


def inner(wanted, here_is, us, share, ys, chips):
    _, size, half = ys[0].shape
    hbm = pl.BlockSpec(memory_space=pltpu.HBM)
    return pl.pallas_call(
        inner_kernel,
        grid_spec=pltpu.PrefetchScalarGridSpec(
            num_scalar_prefetch=2,
            grid=(),
            in_specs=[hbm] * 4 + in_vmem(3),
            out_specs=in_vmem(chips),
            scratch_shapes=[
                pltpu.VMEM((4, *us[0].shape), F32),
                pltpu.VMEM((10 * size, size), F32),
                pltpu.SemaphoreType.DMA((4, ITEMS)),
            ],
        ),
        out_shape=[jax.ShapeDtypeStruct((10 * size // chips, size), F32)] * chips,
        compiler_params=params(36),
        cost_estimate=pl.CostEstimate(
            flops=18 * ITEMS * size * half * half, bytes_accessed=8 * MIB, transcendentals=0
        ),
        name="inner",
    )(wanted, here_is, *us, share, *ys)


def square_kernel(core, mine, oth, out):
    size = mine.shape[1]

    def put(j, row, col, tile):
        out[j, row * size:(row + 1) * size, col * size:(col + 1) * size] = tile

    for j in range(2):
        for c in range(2):
            diag0, below, diag1, one, two = (jnp.where(core[0] == c, mine[5 * j + k], oth[5 * j + k]) for k in range(5))
            put(j, 2 * c, 2 * c, diag0)
            put(j, 2 * c + 1, 2 * c, below)
            put(j, 2 * c, 2 * c + 1, below.T)
            put(j, 2 * c + 1, 2 * c + 1, diag1)
            for t, tile in enumerate((one, two)):
                row, col = (2, t) if c == 0 else (t, 3)
                put(j, row, col, tile)
                put(j, col, row, tile.T)


def square(core, mine, oth):
    size = mine.shape[1]
    return pl.pallas_call(
        square_kernel,
        grid_spec=pltpu.PrefetchScalarGridSpec(
            num_scalar_prefetch=1, grid=(), in_specs=in_vmem(2), out_specs=pl.BlockSpec(memory_space=pltpu.VMEM)
        ),
        out_shape=jax.ShapeDtypeStruct((2, 4 * size, 4 * size), F32),
        compiler_params=params(),
        cost_estimate=pl.CostEstimate(flops=0, bytes_accessed=4 * MIB, transcendentals=0),
        name="square",
    )(core, mine, oth)


def order_kernel(chip, *refs):
    h = refs[0].shape[0]
    for bits, ref in enumerate(refs[:-1]):
        refs[-1][pl.ds(pl.multiple_of((chip[0] ^ bits) * h, 8), h)] = ref[...]


def order(chip, came):
    h, width = came[0].shape
    return pl.pallas_call(
        order_kernel,
        grid_spec=pltpu.PrefetchScalarGridSpec(
            num_scalar_prefetch=1, grid=(), in_specs=in_vmem(len(came)), out_specs=pl.BlockSpec(memory_space=pltpu.VMEM)
        ),
        out_shape=jax.ShapeDtypeStruct((len(came) * h, width), F32),
        compiler_params=params(),
        cost_estimate=pl.CostEstimate(flops=0, bytes_accessed=2 * MIB, transcendentals=0),
        name="order",
    )(chip, *came)


def keep_kernel(*refs):
    count = (len(refs) - 1) // 2
    copies = [pltpu.make_async_copy(refs[k], refs[count + k], refs[-1].at[k]) for k in range(count)]
    for copy in copies:
        copy.start()
    for copy in copies:
        copy.wait()


def keep(*arrays):
    hbm = pl.BlockSpec(memory_space=pltpu.HBM)
    return pl.pallas_call(
        keep_kernel,
        in_specs=in_vmem(len(arrays)),
        out_specs=[hbm] * len(arrays),
        out_shape=[jax.ShapeDtypeStruct(x.shape, x.dtype) for x in arrays],
        scratch_shapes=[pltpu.SemaphoreType.DMA((len(arrays),))],
        compiler_params=params(),
        cost_estimate=pl.CostEstimate(flops=0, bytes_accessed=4 * MIB, transcendentals=0),
        name="keep",
    )(*arrays)


def place_kernel(wanted, core, y0, y1, z0, z1, oth, out):
    rows, half = ITEMS // 2, y0.shape[2]
    part = out.shape[1]
    for step in range(2 * rows // part):

        @pl.when(pl.program_id(0) == step)
        def _():
            j = step * part // rows
            for q in range(step * part % rows, step * part % rows + part):
                keep = wanted[j * rows + q] != 0
                which, at = where_is(j, 0, q, rows)
                mine = jnp.where(keep, -((y0, y1)[which][at] + (z0, z1)[which][at]), 0.0)
                other = jnp.where(keep, -oth[j * rows + q], 0.0)
                out[0, q % part, :, :half] = jnp.where(core[0] == 0, mine, other)
                out[0, q % part, :, half:] = jnp.where(core[0] == 0, other, mine)


def place(wanted, core, ys, recv, oth):
    _, size, half = ys[0].shape
    rows = ITEMS // 2
    return pl.pallas_call(
        place_kernel,
        grid_spec=pltpu.PrefetchScalarGridSpec(
            num_scalar_prefetch=2,
            grid=(4,),
            in_specs=in_vmem(5),
            out_specs=pl.BlockSpec((1, rows // 2, size, 2 * half), lambda i, *_: (i // 2, i % 2, 0, 0)),
        ),
        out_shape=jax.ShapeDtypeStruct((2, rows, size, 2 * half), F32),
        compiler_params=params(),
        cost_estimate=pl.CostEstimate(flops=0, bytes_accessed=5 * MIB, transcendentals=0),
        name="place",
    )(wanted, core, *ys, *recv, oth)


def any_mesh(sigma_anc, panel, pattern, linv):
    high = lax.Precision.HIGH
    einsum = functools.partial(jnp.einsum, precision=high, preferred_element_type=F32)
    rows, cols = lax.axis_size("row"), lax.axis_size("col")
    row_ids = jnp.arange(sigma_anc.shape[0], dtype=jnp.int32) * rows + lax.axis_index("row")
    col_ids = jnp.arange(sigma_anc.shape[1], dtype=jnp.int32) * cols + lax.axis_index("col")
    wanted = jnp.any(pattern[:, :, None] == row_ids, axis=1).astype(F32)[:, :, None, None]
    u = einsum("sqiw,swv->sqiv", panel, linv) * wanted
    pick = (col_ids[:, None] == row_ids[None, :]).astype(F32)
    u_cols = lax.psum(jnp.einsum("kq,sqiw->skiw", pick, u, precision=lax.Precision.HIGHEST), "row")
    y = lax.psum(einsum("qkij,skjw->sqiw", sigma_anc, u_cols), "col") * wanted
    total = lax.psum(einsum("sqiw,sqiv->swv", u, y), "row")
    return -y, einsum("siw,siv->swv", linv, linv) + total


def ring_place(chip, chips):
    z, x = chip // 2, chip % 2
    return jnp.where(x == 0, z, chips - 1 - z)


def ring_chip(place, chips):
    place = place % chips
    return jnp.where(place < chips // 2, 2 * place, 2 * (chips - 1 - place) + 1)


def pair_rows(sigma_anc, panel, linv, wanted):
    supers, rows, size, width = panel.shape
    half = width // 2
    n_row = lax.axis_size("row")
    chips = n_row // 2
    me, plane = lax.axis_index("row"), lax.axis_index("col")
    chip, core = me // 2, me % 2
    place_here = ring_place(chip, chips)
    across = [(i, i ^ 1) for i in range(n_row)]
    pair = [(0, 1), (1, 0)]
    order = [2 * q for q in range(chips // 2)] + [2 * (chips - 1 - q) + 1 for q in range(chips // 2, chips)]
    around = []
    for q in range(chips):
        around.append((2 * order[q], 2 * order[(q + 1) % chips]))
        around.append((2 * order[q] + 1, 2 * order[(q - 1) % chips] + 1))

    near, away = update(core[None], far(panel), far(linv))
    away_oth = lax.ppermute(away, "row", across)
    first = jnp.where(core == plane, near, away_oth)
    wanted_here = jnp.where(plane == 0, wanted[0], wanted[1]).reshape(-1)
    wanted_rows = jnp.where(core == 0, wanted, wanted[::-1])
    wanted_rows = lax.dynamic_index_in_dim(wanted_rows, chip, 1, keepdims=False).reshape(-1)
    held = [first[:rows], first[rows:]]
    accs = [jnp.zeros((count, size, half), F32) for count in (FIRST, 2 * ITEMS - FIRST)]
    span = width // (2 * chips)
    share = lax.dynamic_slice_in_dim(linv, (chip * 2 + plane) * span, span, axis=1)
    waiting = []
    s_own = far(sigma_anc)
    s_oth = near_oth = None
    for step in range(chips):
        origin = ring_chip(place_here + jnp.where(core == 0, -step, step), chips)
        blocks = tuple(held)
        if step < chips - 1:
            came = held[0]
            held[0] = lax.ppermute(came, "row", around)
            while len(waiting) > 1:
                accs = add_columns(*waiting.pop(0), accs)
            if step == 3:
                us = keep(*us)
                wanted_rows, share, held[1], *us = lax.optimization_barrier((wanted_rows, share, held[1], *us))
            sent, _, *accs = lax.optimization_barrier((held[1], came, *accs))
            held[1] = lax.ppermute(sent, "row", around)
        if s_oth is None:
            s_sent, near_sent, _ = lax.optimization_barrier((sigma_anc, near, away_oth))
            s_oth = lax.ppermute(s_sent, "row", across)
            near_oth = lax.ppermute(near_sent, "row", across)
            us = [near, away, away_oth, near_oth]
        waiting.append((wanted_here, origin[None], *blocks, s_own, s_oth))
    for early in waiting[:-2]:
        accs = add_columns(*early, accs)
    accs, kept = add_columns(*waiting[-2], accs, chip_later=waiting[-1][1])
    accs = add_columns(*waiting[-1], accs, blocks=kept)

    parts = inner(wanted_rows, jnp.stack([core, chip]), [us[k] for k in (0, 2, 1, 3)], share, accs, chips)
    total, recv, y_oth = all_sum(parts, accs, chip, chips, pair, across)
    total = total.reshape(-1, size, size)
    total_oth = lax.ppermute(total, "row", across)
    sigma_sj = place(wanted_rows[:ITEMS], core[None], accs, recv, y_oth)
    return sigma_sj, square(core[None], total, total_oth)


def all_sum(parts, ys, chip, chips, pair, across):
    def flip(bits):
        return [(i, i ^ (2 * bits)) for i in range(2 * chips)]

    most = lax.ppermute(ys[0], "col", pair)
    mine = parts[0]
    for bits in range(1, chips):
        mine = mine + lax.ppermute(parts[bits], "row", flip(bits))
    mine, most = lax.optimization_barrier((mine, most))
    mine = mine + lax.ppermute(mine, "col", pair)
    y_oth = lax.ppermute(ys[0][:ITEMS] + most[:ITEMS], "row", across)
    mine, sent, y_oth = lax.optimization_barrier((mine, ys[1], y_oth))
    rest = lax.ppermute(sent, "col", pair)
    came = [mine] + [lax.ppermute(mine, "row", flip(bits)) for bits in range(1, chips)]
    *came, rest = lax.optimization_barrier((*came, rest))
    return order(chip[None], came), (most, rest), y_oth


def local(sigma_anc, panel, pattern, linv):
    n_row, n_col = lax.axis_size("row"), lax.axis_size("col")
    rows = sigma_anc.shape[0]
    supers = panel.shape[0]
    if (n_row, n_col, rows * supers) != (16, 2, ITEMS):
        return any_mesh(sigma_anc, panel, pattern, linv)
    chips = n_row // 2
    e = jnp.arange(ITEMS, dtype=jnp.int32)
    ids = (
        (e % rows)[None, None, :] * n_row
        + 2 * jnp.arange(chips, dtype=jnp.int32)[None, :, None]
        + jnp.arange(2, dtype=jnp.int32)[:, None, None]
    )
    hit = jnp.any(pattern[:, None, None, None, :] == ids[None, ..., None], axis=-1)
    wanted = jnp.where(e // rows == 0, hit[0], hit[1])
    return pair_rows(sigma_anc, panel, linv, wanted.astype(jnp.int32))


def solution(mesh):
    return jax.shard_map(
        local,
        mesh=mesh,
        in_specs=(P("row", "col", None, None), P(None, "row", None, None), P(), P()),
        out_specs=(P(None, "row", None, None), P()),
        check_vma=False,
    )
```

```python
import functools

import jax
import jax.numpy as jnp
from jax import lax
from jax.experimental import pallas as pl
from jax.experimental.pallas import tpu as pltpu
from jax.sharding import PartitionSpec as P

F32 = jnp.float32
BF16 = jnp.bfloat16
MIB = 1 << 20


def split(x):
    hi = x.astype(BF16)
    return hi, (x - hi.astype(F32)).astype(BF16)


def dot3(a, b, a_axis=1, b_axis=0):
    left = jnp.concatenate([a[0], a[1], a[0]], axis=a_axis)
    right = jnp.concatenate([b[0], b[0], b[1]], axis=b_axis)
    dims = (((a_axis,), (b_axis,)), ((), ()))
    return lax.dot_general(left, right, dims, preferred_element_type=F32)


def three(a, b):
    dot = functools.partial(jnp.dot, preferred_element_type=F32)
    return dot(a[0], b[0]) + (dot(a[0], b[1]) + dot(a[1], b[0]))


ITEMS = 8
FIRST = 9


def where_is(j, source, q, rows):
    n = (1 - source) * 2 * rows + j * rows + q
    return (0, n) if n < FIRST else (1, n - FIRST)


def in_vmem(count):
    return [pl.BlockSpec(memory_space=pltpu.VMEM)] * count


def far(x):
    return pltpu.with_memory_space_constraint(x, pltpu.HBM)


def params(mib=24):
    return pltpu.CompilerParams(vmem_limit_bytes=mib * MIB)


def update_kernel(core, panel, linv, near, away, rows_in, low_in, arrived):
    supers, rows, size, width = panel.shape
    half = width // 2
    swapped = core[0] == 1

    def copies(j):
        yield pltpu.make_async_copy(linv.at[j], low_in.at[j], arrived.at[j, rows])
        for q in range(rows):
            yield pltpu.make_async_copy(panel.at[j, q], rows_in.at[j, q], arrived.at[j, q])

    for j in range(supers):
        for copy in copies(j):
            copy.start()
    for j in range(supers):
        for copy in copies(j):
            copy.wait()
        left = split(rows_in[j].reshape(rows * size, width))
        first = three(left, split(low_in[j, :, :half]))
        second = three([x[:, half:] for x in left], split(low_in[j, half:, half:]))
        here, there = jnp.where(swapped, second, first), jnp.where(swapped, first, second)
        near[j * rows:(j + 1) * rows] = here.reshape(rows, size, half)
        away[j * rows:(j + 1) * rows] = there.reshape(rows, size, half)


def update(core, panel, linv):
    supers, rows, size, width = panel.shape
    hbm = pl.BlockSpec(memory_space=pltpu.HBM)
    return pl.pallas_call(
        update_kernel,
        grid_spec=pltpu.PrefetchScalarGridSpec(
            num_scalar_prefetch=1,
            grid=(),
            in_specs=[hbm, hbm],
            out_specs=in_vmem(2),
            scratch_shapes=[
                pltpu.VMEM(panel.shape, F32),
                pltpu.VMEM(linv.shape, F32),
                pltpu.SemaphoreType.DMA((supers, rows + 1)),
            ],
        ),
        out_shape=[jax.ShapeDtypeStruct((ITEMS, size, width // 2), F32)] * 2,
        compiler_params=params(32),
        cost_estimate=pl.CostEstimate(
            flops=6 * supers * rows * size * width * width, bytes_accessed=6 * MIB, transcendentals=0
        ),
        name="update",
    )(core, panel, linv)


def column_kernel(wanted, chip, u0, u1, own, oth, *refs):
    accs, outs, (blocks, arrived) = refs[:2], refs[2:4], refs[4:]
    rows, cols, size, _ = own.shape
    items, _, width = u0.shape

    def copy(i, source):
        ref = (own, oth)[source]
        column = i * (cols // items) + chip[0]
        return pltpu.make_async_copy(ref.at[:, column], blocks.at[i, source], arrived.at[i, source])

    def wants(i):
        at = chip[0] * ITEMS + i
        return wanted[at] != 0, wanted[at + items] != 0

    for i in range(items):
        first, second = wants(i)

        @pl.when(first | second)
        def _():
            copy(i, 0).start()
            copy(i, 1).start()

    for acc, out in zip(accs, outs):
        out[...] = acc[...]

    def body(i, carry):
        first, second = wants(i)

        @pl.when(first | second)
        def _():
            pair = [jnp.where(first, u0[i], 0.0), jnp.where(second, u1[i], 0.0)]
            right = split(jnp.concatenate(pair, axis=1))
            copy(i, 0).wait()
            copy(i, 1).wait()
            left = split(blocks[i].reshape(2 * rows * size, size))
            product = dot3(left, right).reshape(2, rows, size, 2 * width)
            for j in range(2):
                for source in range(2):
                    for q in range(rows):
                        which, at = where_is(j, source, q, rows)
                        outs[which][at] += product[source, q, :, j * width:(j + 1) * width]

        return carry

    lax.fori_loop(0, items, body, 0)


def add_columns(wanted, chip, u0, u1, own, oth, accs):
    items, size, width = u0.shape
    rows = own.shape[0]
    hbm = pl.BlockSpec(memory_space=pltpu.HBM)
    return pl.pallas_call(
        column_kernel,
        grid_spec=pltpu.PrefetchScalarGridSpec(
            num_scalar_prefetch=2,
            grid=(),
            in_specs=in_vmem(2) + [hbm, hbm] + in_vmem(2),
            out_specs=in_vmem(2),
            scratch_shapes=[
                pltpu.VMEM((items, 2, rows, size, size), F32),
                pltpu.SemaphoreType.DMA((items, 2)),
            ],
        ),
        out_shape=[jax.ShapeDtypeStruct(acc.shape, F32) for acc in accs],
        input_output_aliases={6 + i: i for i in range(2)},
        compiler_params=params(24),
        cost_estimate=pl.CostEstimate(
            flops=24 * items * rows * size * size * width, bytes_accessed=6 * MIB, transcendentals=0
        ),
        name="add_columns",
    )(wanted, chip, u0, u1, own, oth, *accs)


def inner_kernel(wanted, here_is, *refs):
    us, (share, y0, y1), outs, (held, tiles, arrived) = refs[:4], refs[4:7], refs[7:15], refs[15:]
    _, size, half = y0.shape
    rows = ITEMS // 2
    core = here_is

    def each(k, j, task):
        for q in range(rows):
            e = j * rows + q
            for source in range(2):

                @pl.when(wanted[source * ITEMS + e] != 0)
                def _():
                    task(pltpu.make_async_copy(us[k + source].at[e], held.at[k + source, e], arrived.at[k + source, e]))

    for j in range(2):
        for k in (0, 2):
            each(k, j, lambda copy: copy.start())

    def stack(j, k, start, begin, end):
        parts = [
            jnp.where(wanted[s * ITEMS + j * rows + q] != 0, held[k + s, j * rows + q, :, begin:end], 0.0)
            for s in range(2)
            for q in range(rows)
        ]
        return split(jnp.concatenate(parts + [start[:, begin:end]], axis=0))

    def put(k, tile):
        tiles[k * size:(k + 1) * size] = tile

    for j in range(2):
        low, high = share[j, :, :half], share[j, :, half:]
        here, there = jnp.where(core[0] == 1, high, low), jnp.where(core[0] == 1, low, high)
        right = []
        for source in range(2):
            for q in range(rows):
                which, at = where_is(j, source, q, rows)
                y = (y0, y1)[which][at]
                right.append(jnp.where(wanted[source * ITEMS + j * rows + q] != 0, y, 0.0))
        right = split(jnp.concatenate(right + [here], axis=0))
        first = 5 * j
        each(0, j, lambda copy: copy.wait())
        diag = dot3(stack(j, 0, here, 0, half), right, 0, 0)
        put(first, diag[:size, :size])
        put(first + 1, diag[size:, :size])
        put(first + 2, diag[size:, size:])
        each(2, j, lambda copy: copy.wait())

        @pl.when(core[0] == 0)
        def _():
            cross = dot3(stack(j, 2, there, 0, size), right, 0, 0)
            put(first + 3, cross[:, :size])
            put(first + 4, cross[:, size:])

        @pl.when(core[0] != 0)
        def _():
            cross = dot3(stack(j, 2, there, 0, half), [x[:, size:] for x in right], 0, 0)
            put(first + 3, cross[:size])
            put(first + 4, cross[size:])

    h = outs[0].shape[0]
    for bits, out in enumerate(outs):
        out[...] = tiles[pl.ds(pl.multiple_of((here_is[1] ^ bits) * h, 8), h)]


def inner(wanted, here_is, us, share, ys, chips):
    _, size, half = ys[0].shape
    hbm = pl.BlockSpec(memory_space=pltpu.HBM)
    return pl.pallas_call(
        inner_kernel,
        grid_spec=pltpu.PrefetchScalarGridSpec(
            num_scalar_prefetch=2,
            grid=(),
            in_specs=[hbm] * 4 + in_vmem(3),
            out_specs=in_vmem(chips),
            scratch_shapes=[
                pltpu.VMEM((4, *us[0].shape), F32),
                pltpu.VMEM((10 * size, size), F32),
                pltpu.SemaphoreType.DMA((4, ITEMS)),
            ],
        ),
        out_shape=[jax.ShapeDtypeStruct((10 * size // chips, size), F32)] * chips,
        compiler_params=params(36),
        cost_estimate=pl.CostEstimate(
            flops=18 * ITEMS * size * half * half, bytes_accessed=8 * MIB, transcendentals=0
        ),
        name="inner",
    )(wanted, here_is, *us, share, *ys)


def square_kernel(core, mine, oth, out):
    size = mine.shape[1]

    def put(j, row, col, tile):
        out[j, row * size:(row + 1) * size, col * size:(col + 1) * size] = tile

    for j in range(2):
        for c in range(2):
            diag0, below, diag1, one, two = (jnp.where(core[0] == c, mine[5 * j + k], oth[5 * j + k]) for k in range(5))
            put(j, 2 * c, 2 * c, diag0)
            put(j, 2 * c + 1, 2 * c, below)
            put(j, 2 * c, 2 * c + 1, below.T)
            put(j, 2 * c + 1, 2 * c + 1, diag1)
            for t, tile in enumerate((one, two)):
                row, col = (2, t) if c == 0 else (t, 3)
                put(j, row, col, tile)
                put(j, col, row, tile.T)


def square(core, mine, oth):
    size = mine.shape[1]
    return pl.pallas_call(
        square_kernel,
        grid_spec=pltpu.PrefetchScalarGridSpec(
            num_scalar_prefetch=1, grid=(), in_specs=in_vmem(2), out_specs=pl.BlockSpec(memory_space=pltpu.VMEM)
        ),
        out_shape=jax.ShapeDtypeStruct((2, 4 * size, 4 * size), F32),
        compiler_params=params(),
        cost_estimate=pl.CostEstimate(flops=0, bytes_accessed=4 * MIB, transcendentals=0),
        name="square",
    )(core, mine, oth)


def order_kernel(chip, *refs):
    h = refs[0].shape[0]
    for bits, ref in enumerate(refs[:-1]):
        refs[-1][pl.ds(pl.multiple_of((chip[0] ^ bits) * h, 8), h)] = ref[...]


def order(chip, came):
    h, width = came[0].shape
    return pl.pallas_call(
        order_kernel,
        grid_spec=pltpu.PrefetchScalarGridSpec(
            num_scalar_prefetch=1, grid=(), in_specs=in_vmem(len(came)), out_specs=pl.BlockSpec(memory_space=pltpu.VMEM)
        ),
        out_shape=jax.ShapeDtypeStruct((len(came) * h, width), F32),
        compiler_params=params(),
        cost_estimate=pl.CostEstimate(flops=0, bytes_accessed=2 * MIB, transcendentals=0),
        name="order",
    )(chip, *came)


def place_kernel(wanted, core, y0, y1, z0, z1, oth, out):
    rows, half = ITEMS // 2, y0.shape[2]
    part = out.shape[1]
    for step in range(2 * rows // part):

        @pl.when(pl.program_id(0) == step)
        def _():
            j = step * part // rows
            for q in range(step * part % rows, step * part % rows + part):
                keep = wanted[j * rows + q] != 0
                which, at = where_is(j, 0, q, rows)
                mine = jnp.where(keep, -((y0, y1)[which][at] + (z0, z1)[which][at]), 0.0)
                other = jnp.where(keep, -oth[j * rows + q], 0.0)
                out[0, q % part, :, :half] = jnp.where(core[0] == 0, mine, other)
                out[0, q % part, :, half:] = jnp.where(core[0] == 0, other, mine)


def place(wanted, core, ys, recv, oth):
    _, size, half = ys[0].shape
    rows = ITEMS // 2
    return pl.pallas_call(
        place_kernel,
        grid_spec=pltpu.PrefetchScalarGridSpec(
            num_scalar_prefetch=2,
            grid=(4,),
            in_specs=in_vmem(5),
            out_specs=pl.BlockSpec((1, rows // 2, size, 2 * half), lambda i, *_: (i // 2, i % 2, 0, 0)),
        ),
        out_shape=jax.ShapeDtypeStruct((2, rows, size, 2 * half), F32),
        compiler_params=params(),
        cost_estimate=pl.CostEstimate(flops=0, bytes_accessed=5 * MIB, transcendentals=0),
        name="place",
    )(wanted, core, *ys, *recv, oth)


def any_mesh(sigma_anc, panel, pattern, linv):
    high = lax.Precision.HIGH
    einsum = functools.partial(jnp.einsum, precision=high, preferred_element_type=F32)
    rows, cols = lax.axis_size("row"), lax.axis_size("col")
    row_ids = jnp.arange(sigma_anc.shape[0], dtype=jnp.int32) * rows + lax.axis_index("row")
    col_ids = jnp.arange(sigma_anc.shape[1], dtype=jnp.int32) * cols + lax.axis_index("col")
    wanted = jnp.any(pattern[:, :, None] == row_ids, axis=1).astype(F32)[:, :, None, None]
    u = einsum("sqiw,swv->sqiv", panel, linv) * wanted
    pick = (col_ids[:, None] == row_ids[None, :]).astype(F32)
    u_cols = lax.psum(jnp.einsum("kq,sqiw->skiw", pick, u, precision=lax.Precision.HIGHEST), "row")
    y = lax.psum(einsum("qkij,skjw->sqiw", sigma_anc, u_cols), "col") * wanted
    total = lax.psum(einsum("sqiw,sqiv->swv", u, y), "row")
    return -y, einsum("siw,siv->swv", linv, linv) + total


def ring_place(chip, chips):
    z, x = chip // 2, chip % 2
    return jnp.where(x == 0, z, chips - 1 - z)


def ring_chip(place, chips):
    place = place % chips
    return jnp.where(place < chips // 2, 2 * place, 2 * (chips - 1 - place) + 1)


def pair_rows(sigma_anc, panel, linv, wanted):
    supers, rows, size, width = panel.shape
    half = width // 2
    n_row = lax.axis_size("row")
    chips = n_row // 2
    me, plane = lax.axis_index("row"), lax.axis_index("col")
    chip, core = me // 2, me % 2
    place_here = ring_place(chip, chips)
    across = [(i, i ^ 1) for i in range(n_row)]
    pair = [(0, 1), (1, 0)]
    order = [2 * q for q in range(chips // 2)] + [2 * (chips - 1 - q) + 1 for q in range(chips // 2, chips)]
    around = []
    for q in range(chips):
        around.append((2 * order[q], 2 * order[(q + 1) % chips]))
        around.append((2 * order[q] + 1, 2 * order[(q - 1) % chips] + 1))

    near, away = update(core[None], far(panel), far(linv))
    away_oth = lax.ppermute(away, "row", across)
    first = jnp.where(core == plane, near, away_oth)
    wanted_here = jnp.where(plane == 0, wanted[0], wanted[1]).reshape(-1)
    wanted_rows = jnp.where(core == 0, wanted, wanted[::-1])
    wanted_rows = lax.dynamic_index_in_dim(wanted_rows, chip, 1, keepdims=False).reshape(-1)
    held = [first[:rows], first[rows:]]
    accs = [jnp.zeros((count, size, half), F32) for count in (FIRST, 2 * ITEMS - FIRST)]
    span = width // (2 * chips)
    share = lax.dynamic_slice_in_dim(linv, (chip * 2 + plane) * span, span, axis=1)
    waiting = []
    s_own = far(sigma_anc)
    s_oth = near_oth = None
    for step in range(chips):
        origin = ring_chip(place_here + jnp.where(core == 0, -step, step), chips)
        blocks = tuple(held)
        if step < chips - 1:
            came = held[0]
            held[0] = lax.ppermute(came, "row", around)
            while len(waiting) > 1:
                accs = add_columns(*waiting.pop(0), accs)
            if step == 3:
                us = [far(u) for u in us]
                wanted_rows, share, held[1], *us = lax.optimization_barrier((wanted_rows, share, held[1], *us))
            sent, _, *accs = lax.optimization_barrier((held[1], came, *accs))
            held[1] = lax.ppermute(sent, "row", around)
        if s_oth is None:
            s_sent, near_sent, _ = lax.optimization_barrier((sigma_anc, near, away_oth))
            s_oth = lax.ppermute(s_sent, "row", across)
            near_oth = lax.ppermute(near_sent, "row", across)
            us = [near, away, away_oth, near_oth]
        waiting.append((wanted_here, origin[None], *blocks, s_own, s_oth))
    for last in waiting:
        accs = add_columns(*last, accs)

    parts = inner(wanted_rows, jnp.stack([core, chip]), [us[k] for k in (0, 2, 1, 3)], share, accs, chips)
    total, recv, y_oth = all_sum(parts, accs, chip, chips, pair, across)
    total = total.reshape(-1, size, size)
    total_oth = lax.ppermute(total, "row", across)
    total_oth, rest = lax.optimization_barrier((total_oth, recv[1]))
    recv = (recv[0], rest)
    sigma_sj = place(wanted_rows[:ITEMS], core[None], accs, recv, y_oth)
    return sigma_sj, square(core[None], total, total_oth)


def all_sum(parts, ys, chip, chips, pair, across):
    def flip(bits):
        return [(i, i ^ (2 * bits)) for i in range(2 * chips)]

    most = lax.ppermute(ys[0], "col", pair)
    mine = parts[0]
    for bits in range(1, chips):
        mine = mine + lax.ppermute(parts[bits], "row", flip(bits))
    mine, most = lax.optimization_barrier((mine, most))
    mine = mine + lax.ppermute(mine, "col", pair)
    y_oth = lax.ppermute(ys[0][:ITEMS] + most[:ITEMS], "row", across)
    mine, sent, y_oth = lax.optimization_barrier((mine, ys[1], y_oth))
    rest = lax.ppermute(sent, "col", pair)
    came = [mine] + [lax.ppermute(mine, "row", flip(bits)) for bits in range(1, chips)]
    return order(chip[None], came), (most, rest), y_oth


def local(sigma_anc, panel, pattern, linv):
    n_row, n_col = lax.axis_size("row"), lax.axis_size("col")
    rows = sigma_anc.shape[0]
    supers = panel.shape[0]
    if (n_row, n_col, rows * supers) != (16, 2, ITEMS):
        return any_mesh(sigma_anc, panel, pattern, linv)
    chips = n_row // 2
    e = jnp.arange(ITEMS, dtype=jnp.int32)
    ids = (
        (e % rows)[None, None, :] * n_row
        + 2 * jnp.arange(chips, dtype=jnp.int32)[None, :, None]
        + jnp.arange(2, dtype=jnp.int32)[:, None, None]
    )
    hit = jnp.any(pattern[:, None, None, None, :] == ids[None, ..., None], axis=-1)
    wanted = jnp.where(e // rows == 0, hit[0], hit[1])
    return pair_rows(sigma_anc, panel, linv, wanted.astype(jnp.int32))


def solution(mesh):
    return jax.shard_map(
        local,
        mesh=mesh,
        in_specs=(P("row", "col", None, None), P(None, "row", None, None), P(), P()),
        out_specs=(P(None, "row", None, None), P()),
        check_vma=False,
    )
```
